128 devices in a mesh: dp: 8 (over z, core), ctx: 16 (over x, y).
Axes of the slice: x: 4, y: 4, z: 4, core: 2. Of those that a mesh axis runs over, the one named last changes fastest.
Arguments:
- query_rows: bfloat16 [16384, 4096], P(('dp', 'ctx')), may hold values from -8 to 8
- key_rows: bfloat16 [16384, 512], P(('dp', 'ctx')), may hold values from -8 to 8
- value_rows: bfloat16 [16384, 512], P(('dp', 'ctx')), may hold values from -6 to 6
- grad_out: bfloat16 [16384, 4096], P(('dp', 'ctx')), may hold values from -6 to 6
- send_order: int32 [8, 16, 128], P('dp', 'ctx'), may hold values from 0 to 127, each once within a row
- recv_place: int32 [8, 16, 128], P('dp', 'ctx'), may hold values from 0 to 127, each once within a row
- doc_ids: int32 [8, 2048], P('dp'), may hold values from 0 to 7, never falling along the last dimension, each value on 1 to 1024 neighbouring positions
Outputs:
- attn_out: bfloat16 [16384, 4096], P(('dp', 'ctx'))
- grad_queries: bfloat16 [16384, 4096], P(('dp', 'ctx'))
- grad_keys: bfloat16 [16384, 512], P(('dp', 'ctx'))
- grad_values: bfloat16 [16384, 512], P(('dp', 'ctx'))
The draws below stay inside these ranges and needn't reach their ends.
Inputs may be any that keep to these rules, and one draw needn't show every extreme that they name: `send_order`: each row of a device is a permutation of its 128 slots. `recv_place`: each row of a device is a permutation of its 128 slots. `doc_ids`: never falling along a row; a document holds at most 1024 positions and one in each row holds exactly that many.
All inputs are finite; a program needn't handle non-finite values.
Results may differ from the reference program's by a relative error of at most 0.035.
Values may be sent and summed in bfloat16 or wider, within the bound.
A program may use at most 128 MiB of HBM per device.

```python
import math
import jax
import jax.numpy as jnp
import numpy as np
from jax import lax

HEADS = 32
KV_HEADS = 4
HEAD_DIM = 128
TOK_DEV = 128
DOCS = 8
SEQ = 2048
DOC_MOST = 1024
TOKENS = 16384
N_DP = 8
N_CTX = 16


def draw_query_rows(key, part):
    key = jax.random.fold_in(key, 1)
    noise_key = jax.random.fold_in(key, 0)
    values = jax.random.truncated_normal(noise_key, -4.0, 4.0, (TOKENS, HEADS, HEAD_DIM), jnp.float32)
    return values.reshape(TOKENS, HEADS * HEAD_DIM).astype(jnp.bfloat16)


def draw_key_rows(key, part):
    key = jax.random.fold_in(key, 2)
    noise_key = jax.random.fold_in(key, 0)
    values = jax.random.truncated_normal(noise_key, -4.0, 4.0, (TOKENS, KV_HEADS, HEAD_DIM), jnp.float32)
    return values.reshape(TOKENS, KV_HEADS * HEAD_DIM).astype(jnp.bfloat16)


def block_levels(key, dims, cuts, least, high):
    gain = 1.0
    for position, blocks in cuts:
        steps = jax.random.uniform(jax.random.fold_in(jax.random.fold_in(key, 6), position), (blocks,), jnp.float32, least / len(cuts), high / len(cuts))
        gain = gain * jnp.repeat(jnp.exp(steps), dims[position] // blocks).reshape((-1,) + (1,) * (len(dims) - 1 - position))
    return gain


def split_up(number_of, total, bound, lean):
    weights = [(1 << 20) // math.isqrt(grade ** lean) + 1 for grade in range(2, number_of + 1)]
    surplus, counts = total - bound - (number_of - 1), [1] * (number_of - 1)
    while surplus > 0:
        free = [i for i in range(number_of - 1) if counts[i] < bound]
        pool, remaining = sum([weights[i] for i in free]), surplus
        for i in free:
            addition = min(bound - counts[i], max(1, remaining * weights[i] // pool), surplus)
            counts[i] = counts[i] + addition
            surplus = surplus - addition
    return np.array([bound] + counts)


def uneven(key, amount, total, limit, slope):
    if amount == 2:
        one = jax.random.randint(key, (), max(1, total - limit), min(limit, total - 1) + 1)
        return jnp.stack([one, total - one])
    sizes = jnp.asarray(split_up(amount, total, limit, slope), jnp.int32)
    twos = (amount - 1) // 2
    donor, sink = sizes[1:1 + 2 * twos:2], sizes[2:2 + 2 * twos:2]
    room = jnp.minimum(donor - 1, limit - sink)
    shifted = jax.random.randint(jax.random.fold_in(key, 1), (twos,), 0, 1 << 20) % (room + 1)
    sizes = sizes.at[1:1 + 2 * twos:2].set(donor - shifted).at[2:2 + 2 * twos:2].set(sink + shifted)
    return sizes[jax.random.permutation(jax.random.fold_in(key, 2), amount)]


def bell_draw(key, shape, scale, bound, shards=(), kind=jnp.bfloat16):
    values = jax.random.normal(key, shape, jnp.float32) * scale
    if len(shards) > 0:
        values = block_levels(key, shape, shards, -0.22, 0.18) * values
    return jnp.clip(values, min=-bound, max=bound).astype(kind)


def setup_inputs(seed: int = 0) -> dict:
    arg_keys = jax.random.split(jax.random.key(seed), 8)
    query_rows = draw_query_rows(jax.random.fold_in(arg_keys[7], 71), 0)
    key_rows = draw_key_rows(jax.random.fold_in(arg_keys[7], 71), 0)
    value_rows = bell_draw(arg_keys[2], (TOKENS, KV_HEADS * HEAD_DIM), 1.0, 6.0, ((0, 128),))
    grad_out = bell_draw(arg_keys[3], (TOKENS, HEADS * HEAD_DIM), 1.0, 6.0, ((0, 128),))
    send_order = jax.vmap(lambda own: jax.random.permutation(own, TOK_DEV))(jax.random.split(arg_keys[4], N_DP * N_CTX)).reshape((N_DP, N_CTX, TOK_DEV)).astype(jnp.int32)
    recv_place = jax.vmap(lambda own: jax.random.permutation(own, TOK_DEV))(jax.random.split(arg_keys[5], N_DP * N_CTX)).reshape((N_DP, N_CTX, TOK_DEV)).astype(jnp.int32)
    doc_ids = jax.vmap(lambda own: jnp.searchsorted(jnp.cumsum(uneven(own, DOCS, SEQ, DOC_MOST, 2)), jnp.arange(SEQ), side="right"))(jax.random.split(arg_keys[6], N_DP)).reshape((N_DP, SEQ)).astype(jnp.int32)
    return {"query_rows": query_rows, "key_rows": key_rows, "value_rows": value_rows, "grad_out": grad_out, "send_order": send_order, "recv_place": recv_place, "doc_ids": doc_ids}


def to_owners(matrix, send_order, recv_place):
    width = matrix.shape[-1]
    share = TOK_DEV // N_DP
    grouped = matrix.reshape(N_DP, N_CTX, TOK_DEV, width)
    outgoing = jnp.take_along_axis(grouped, send_order[..., None], axis=2)
    arrived = outgoing.reshape(N_DP, N_CTX, N_DP, share, width).transpose(2, 1, 0, 3, 4).reshape(N_DP, N_CTX, TOK_DEV, width)
    inverse = jnp.argsort(recv_place, axis=-1).astype(jnp.int32)
    placed = jnp.take_along_axis(arrived, inverse[..., None], axis=2)
    return placed.reshape(N_DP, SEQ, width)


def to_home(matrix, send_order, recv_place):
    width = matrix.shape[-1]
    share = TOK_DEV // N_DP
    grouped = matrix.reshape(N_DP, N_CTX, TOK_DEV, width)
    slots = jnp.take_along_axis(grouped, recv_place[..., None], axis=2)
    returned = slots.reshape(N_DP, N_CTX, N_DP, share, width).transpose(2, 1, 0, 3, 4).reshape(N_DP, N_CTX, TOK_DEV, width)
    inverse = jnp.argsort(send_order, axis=-1).astype(jnp.int32)
    homed = jnp.take_along_axis(returned, inverse[..., None], axis=2)
    return homed.reshape(TOKENS, width)


def head_pass(query_head, key_head, value_head, grad_head, allowed):
    scaling = HEAD_DIM ** -0.5
    query_wide = query_head.astype(jnp.float32)
    key_wide = key_head.astype(jnp.float32)
    value_wide = value_head.astype(jnp.float32)
    grad_wide = grad_head.astype(jnp.float32)
    scores = jnp.einsum('igd,jd->gij', query_wide, key_wide) * scaling
    row_max = jnp.max(jnp.where(allowed, scores, -jnp.inf), axis=-1)
    row_sum = jnp.sum(jnp.where(allowed, jnp.exp(scores - row_max[..., None]), 0.0), axis=-1)
    log_total = row_max + jnp.log(row_sum)
    weights = jnp.where(allowed, jnp.exp(scores - log_total[..., None]), 0.0)
    weights_b = weights.astype(jnp.bfloat16).astype(jnp.float32)
    out_head = jnp.einsum('gij,jd->igd', weights_b, value_wide).astype(jnp.bfloat16)
    row_delta = jnp.sum(grad_wide * out_head.astype(jnp.float32), axis=-1).T
    prob_grad = jnp.einsum('igd,jd->gij', grad_wide, value_wide)
    dscore = (weights * (prob_grad - row_delta[..., None])).astype(jnp.bfloat16).astype(jnp.float32)
    grad_query = (scaling * jnp.einsum('gij,jd->igd', dscore, key_wide)).astype(jnp.bfloat16)
    grad_key = (scaling * jnp.einsum('gij,igd->jd', dscore, query_wide)).astype(jnp.bfloat16)
    grad_value = jnp.einsum('gij,igd->jd', weights_b, grad_wide).astype(jnp.bfloat16)
    return out_head, grad_query, grad_key, grad_value


def group_pass(query_group, key_group, value_group, grad_group, doc_row):
    positions = jnp.arange(SEQ, dtype=jnp.int32)
    allowed = (doc_row[:, None] == doc_row[None, :]) & (positions[None, :] <= positions[:, None])
    group_size = HEADS // KV_HEADS
    query_heads = query_group.reshape(SEQ, KV_HEADS, group_size, HEAD_DIM).transpose(1, 0, 2, 3)
    grad_heads = grad_group.reshape(SEQ, KV_HEADS, group_size, HEAD_DIM).transpose(1, 0, 2, 3)
    key_heads = key_group.reshape(SEQ, KV_HEADS, HEAD_DIM).transpose(1, 0, 2)
    value_heads = value_group.reshape(SEQ, KV_HEADS, HEAD_DIM).transpose(1, 0, 2)
    out_heads, dq_heads, dk_heads, dv_heads = lax.map(lambda inputs: head_pass(inputs[0], inputs[1], inputs[2], inputs[3], allowed), (query_heads, key_heads, value_heads, grad_heads))
    out_group = out_heads.transpose(1, 0, 2, 3).reshape(SEQ, HEADS * HEAD_DIM)
    dq_group = dq_heads.transpose(1, 0, 2, 3).reshape(SEQ, HEADS * HEAD_DIM)
    dk_group = dk_heads.transpose(1, 0, 2).reshape(SEQ, KV_HEADS * HEAD_DIM)
    dv_group = dv_heads.transpose(1, 0, 2).reshape(SEQ, KV_HEADS * HEAD_DIM)
    return out_group, dq_group, dk_group, dv_group


def reference(query_rows, key_rows, value_rows, grad_out, send_order, recv_place, doc_ids):
    query_att = to_owners(query_rows, send_order, recv_place)
    key_att = to_owners(key_rows, send_order, recv_place)
    value_att = to_owners(value_rows, send_order, recv_place)
    grad_att = to_owners(grad_out, send_order, recv_place)
    out_att, dq_att, dk_att, dv_att = lax.map(lambda inputs: group_pass(inputs[0], inputs[1], inputs[2], inputs[3], inputs[4]), (query_att, key_att, value_att, grad_att, doc_ids))
    return (to_home(out_att, send_order, recv_place), to_home(dq_att, send_order, recv_place), to_home(dk_att, send_order, recv_place), to_home(dv_att, send_order, recv_place))
```

```python
import jax
import jax.numpy as jnp
from jax import lax
from jax.experimental import pallas as pl
from jax.experimental.pallas import tpu as pltpu
from jax.sharding import PartitionSpec as P

BF, F32, I32 = jnp.bfloat16, jnp.float32, jnp.int32
MESH = pl.DeviceIdType.MESH
HD = 128
KH = 4
GS = 8
T = 128
NDP = 8
SHARE = T // NDP
NCH = 9
W = NCH * T
GW = GS * HD
SCALE = HD**-0.5
SCALE2 = SCALE * 1.4426950408889634
NEG = -1e30
NT = (((1,), (1,)), ((), ()))
NN = (((1,), (0,)), ((), ()))


def dot(a, b, dims=NN):
    return lax.dot_general(a, b, dims, preferred_element_type=F32)


def kernel(
    q_hbm, k_hbm, v_hbm, g_hbm, order_ref, place_ref, doc_ref,
    out_hbm, dq_hbm, dk_hbm, dv_hbm,
    q_in, g_in, k_in, v_in, hot, hot_t, nat, nat_t,
    kvs, kvr, qgs, qgr, kv, bias, kt, vt,
    ods, odr, dkv, yrec, acc, xs, xrec, zks, zkr, home, gk, gv,
    in_sem, out_sem, kv_ss, kv_rs, qg_ss, qg_rs, x_ss, x_rs, y_ss, y_rs,
    od_ss, od_rs, yr_ss, yr_rs, xr_ss, xr_rs, zk_ss, zk_rs,
):
    d = lax.axis_index("dp")
    c = lax.axis_index("ctx")
    x, y = c // 4, c % 4

    def group_at(j):
        return (lax.rem(d + j, NDP), c)

    def x_at(j):
        return (d, lax.rem(x + j + 4, 4) * 4 + y)

    def y_at(j):
        return (d, x * 4 + lax.rem(y + j + 4, 4))

    bar = pltpu.get_barrier_semaphore()
    friends = [group_at(j) for j in range(1, NDP)]
    friends += [x_at(j) for j in range(1, 4)] + [y_at(j) for j in range(1, 4)]
    for f in friends:
        pl.semaphore_signal(bar, 1, device_id=f, device_id_type=MESH)

    k_cp = pltpu.make_async_copy(k_hbm, k_in, in_sem.at[0])
    v_cp = pltpu.make_async_copy(v_hbm, v_in, in_sem.at[1])
    q_cp = pltpu.make_async_copy(q_hbm, q_in, in_sem.at[2])
    g_cp = pltpu.make_async_copy(g_hbm, g_in, in_sem.at[3])
    for cp in (k_cp, v_cp, q_cp, g_cp):
        cp.start()

    rows = lax.broadcasted_iota(I32, (T, T), 0)
    hot_t32 = (rows == order_ref[...]).astype(F32)
    nat32 = (rows == place_ref[...]).astype(F32)
    hot_t[...] = hot_t32.astype(BF)
    hot[...] = hot_t32.T.astype(BF)
    nat[...] = nat32.astype(BF)
    nat_t[...] = nat32.T.astype(BF)

    mine = pl.ds(pl.multiple_of(d * SHARE, SHARE), SHARE)

    def part(j):
        return pl.ds(pl.multiple_of(lax.rem(d + j, NDP) * SHARE, SHARE), SHARE)

    def rcopy(src, dst, ss, rs, to):
        return pltpu.make_async_remote_copy(
            src_ref=src, dst_ref=dst, send_sem=ss, recv_sem=rs, device_id=to, device_id_type=MESH
        )

    def kv_copy(j):
        return rcopy(kvs.at[part(j)], kvr.at[mine], kv_ss.at[j], kv_rs.at[j], group_at(j))

    def qg_copy(g, j):
        return rcopy(
            qgs.at[g, part(j)], qgr.at[g, mine], qg_ss.at[g, j], qg_rs.at[g, j], group_at(j)
        )

    def od_copy(g, j):
        return rcopy(
            ods.at[g, part(j)], odr.at[g, mine], od_ss.at[g, j], od_rs.at[g, j], group_at(j)
        )

    def zk_copy(g, j):
        return rcopy(
            zks.at[g, part(j)], zkr.at[g, mine], zk_ss.at[g, j], zk_rs.at[g, j], group_at(j)
        )

    def chunk(o):
        return pl.ds(pl.multiple_of(o * T, T), T)

    def x_copy(g, j):
        return rcopy(
            kv.at[g, chunk(0)], kv.at[g, chunk(4 * j)], x_ss.at[g, j], x_rs.at[g, j], x_at(j)
        )

    def y_copy(g, j, b):
        turn = (y + j) // 4
        return rcopy(
            kv.at[g, chunk(4 * (turn + b))], kv.at[g, chunk(j + 4 * b)],
            y_ss.at[g, j, b], y_rs.at[g, j, b], y_at(j),
        )

    def yr_copy(g, j, b):
        return rcopy(
            dkv.at[g, chunk(j + 4 * b)], yrec.at[g, j - 1, b],
            yr_ss.at[g, j, b], yr_rs.at[g, j, b], y_at(-j),
        )

    def xr_copy(g, j):
        return rcopy(
            xs.at[g, j - 1], xrec.at[g, j - 1], xr_ss.at[g, j], xr_rs.at[g, j], x_at(-j)
        )

    k_cp.wait()
    v_cp.wait()
    for g in range(KH):
        cols = slice(g * HD, (g + 1) * HD)
        kvs[:, 2 * g * HD : (2 * g + 1) * HD] = dot(hot[...], k_in[:, cols]).astype(BF)
        kvs[:, (2 * g + 1) * HD : (2 * g + 2) * HD] = dot(hot[...], v_in[:, cols]).astype(BF)
    kvr[mine, :] = kvs[mine, :]
    pl.semaphore_wait(bar, len(friends))
    for j in range(1, NDP):
        kv_copy(j).start()

    q_cp.wait()
    g_cp.wait()

    def send_rows(g, carry):
        cols = pl.ds(pl.multiple_of(g * GW, GW), GW)
        qgs[g, :, 0:GW] = dot(hot[...], q_in[:, cols]).astype(BF)
        qgs[g, :, GW : 2 * GW] = dot(hot[...], g_in[:, cols]).astype(BF)
        qgr[g, mine, :] = qgs[g, mine, :]
        for j in range(1, NDP):
            qg_copy(g, j).start()
        return carry

    lax.fori_loop(0, KH, send_rows, 0)

    q_pos = place_ref[...]
    own_doc = doc_ref[0:1, pl.ds(pl.multiple_of(c * T, T), T)].astype(F32).astype(BF)
    q_doc = dot(jnp.broadcast_to(own_doc, (8, T)), nat[...])[0:1]

    def mask(o, carry):
        at = lax.rem(c - o + 16, 16)
        row = doc_ref[0:1, pl.ds(pl.multiple_of(at * T, T), T)].astype(F32)
        k_doc = jnp.broadcast_to(row, (T, T)).T
        ahead = jnp.where(o == 0, rows - q_pos, 0)
        ahead = jnp.where(o <= c, ahead, 1)
        bias[chunk(o), :] = jnp.where((k_doc == q_doc) & (ahead <= 0), 0.0, NEG)
        return carry

    lax.fori_loop(0, NCH, mask, 0)

    for j in range(1, NDP):
        kv_copy(j).wait_recv()
    for g in range(KH):
        cols = slice(2 * g * HD, 2 * (g + 1) * HD)
        kv[g, 0:T, :] = dot(nat[...], kvr[:, cols]).astype(BF)
        for j in (1, 2):
            x_copy(g, j).start()

    def pass_on(g):
        for j in (1, 2):
            x_copy(g, j).wait_recv()
        for j in (1, 2, 3):
            for b in (0, 1):
                y_copy(g, j, b).start()

    for g in range(3):
        pass_on(g)

    def attend(g):
        for j in range(1, NDP):
            qg_copy(g, j).wait_recv()
        for j in (1, 2, 3):
            for b in (0, 1):
                y_copy(g, j, b).wait_recv()
        keys, values = kv[g, :, 0:HD], kv[g, :, HD : 2 * HD]
        kt[...] = keys.T
        vt[...] = values.T
        query = jnp.concatenate([qgr[g, :, h * HD : (h + 1) * HD] for h in range(GS)], axis=0)
        grad = jnp.concatenate(
            [qgr[g, :, GW + h * HD : GW + (h + 1) * HD] for h in range(GS)], axis=0
        )
        scores = dot(keys, query, NT) * SCALE2 + jnp.concatenate([bias[...]] * GS, axis=1)
        weights = jnp.exp2(scores - jnp.max(scores, axis=0, keepdims=True))
        probs = weights * (1.0 / jnp.sum(weights, axis=0, keepdims=True))
        probs_b = probs.astype(BF)
        out = dot(vt[...], probs_b).astype(BF)
        prob_grad = dot(values, grad, NT)
        delta = jnp.sum(out.astype(F32) * grad.T.astype(F32), axis=0, keepdims=True)
        dscore = (probs * (prob_grad - delta)).astype(BF)
        dq = (dot(kt[...], dscore) * SCALE).astype(BF)
        out, dq = out.T, dq.T
        for h in range(GS):
            ods[g, :, h * HD : (h + 1) * HD] = out[h * T : (h + 1) * T]
            ods[g, :, GW + h * HD : GW + (h + 1) * HD] = dq[h * T : (h + 1) * T]
        dkv[g, :, 0:HD] = (dot(dscore, query) * SCALE).astype(BF)
        dkv[g, :, HD : 2 * HD] = dot(probs_b, grad).astype(BF)
        odr[g, mine, :] = ods[g, mine, :]
        for j in (1, 2, 3):
            for b in (0, 1):
                yr_copy(g, j, b).start()
        for j in range(1, NDP):
            od_copy(g, j).start()

    def add_y(g):
        for k in range(3):
            acc[g, k] = dkv[g, 4 * k * T : (4 * k + 1) * T, :].astype(F32)
        for j in (1, 2, 3):
            turn = (y + j) // 4
            for b in (0, 1):
                yr_copy(g, j, b).wait_recv()
                acc[g, turn + b] += yrec[g, j - 1, b].astype(F32)
        for j in (1, 2):
            xs[g, j - 1] = acc[g, j].astype(BF)
            xr_copy(g, j).start()

    def add_x(g):
        total = acc[g, 0]
        for j in (1, 2):
            xr_copy(g, j).wait_recv()
            total += xrec[g, j - 1].astype(F32)
        zks[g] = dot(nat_t[...], total.astype(BF)).astype(BF)
        zkr[g, mine, :] = zks[g, mine, :]
        for j in range(1, NDP):
            zk_copy(g, j).start()

    def home_copies(g):
        cols = pl.ds(pl.multiple_of(g * GW, GW), GW)
        return (
            pltpu.make_async_copy(home.at[g, :, 0:GW], out_hbm.at[:, cols], out_sem.at[g, 0]),
            pltpu.make_async_copy(home.at[g, :, GW : 2 * GW], dq_hbm.at[:, cols], out_sem.at[g, 1]),
        )

    def come_home(g):
        for j in range(1, NDP):
            od_copy(g, j).wait_recv()
        home[g] = dot(hot_t[...], odr[g]).astype(BF)
        for cp in home_copies(g):
            cp.start()

    def turn(t, carry):
        @pl.when(t < KH)
        def _():
            attend(t)

        @pl.when(t == 0)
        def _():
            pass_on(3)

        @pl.when((t >= 1) & (t <= KH))
        def _():
            add_y(t - 1)

        @pl.when(t >= 2)
        def _():
            add_x(t - 2)
            come_home(t - 2)

        return carry

    lax.fori_loop(0, KH + 2, turn, 0)

    for g in range(KH):
        for j in range(1, NDP):
            zk_copy(g, j).wait_recv()
        grads = dot(hot_t[...], zkr[g]).astype(BF)
        gk[:, g * HD : (g + 1) * HD] = grads[:, 0:HD]
        gv[:, g * HD : (g + 1) * HD] = grads[:, HD : 2 * HD]
    gk_cp = pltpu.make_async_copy(gk, dk_hbm, in_sem.at[0])
    gv_cp = pltpu.make_async_copy(gv, dv_hbm, in_sem.at[1])
    gk_cp.start()
    gv_cp.start()

    for j in range(1, NDP):
        kv_copy(j).wait_send()

    def drain(g, carry):
        for j in range(1, NDP):
            qg_copy(g, j).wait_send()
            od_copy(g, j).wait_send()
            zk_copy(g, j).wait_send()
        for j in (1, 2):
            x_copy(g, j).wait_send()
            xr_copy(g, j).wait_send()
        for j in (1, 2, 3):
            for b in (0, 1):
                y_copy(g, j, b).wait_send()
                yr_copy(g, j, b).wait_send()
        for cp in home_copies(g):
            cp.wait()
        return carry

    lax.fori_loop(0, KH, drain, 0)
    gk_cp.wait()
    gv_cp.wait()


def body(query_rows, key_rows, value_rows, grad_out, send_order, recv_place, doc_ids):
    vm = pltpu.VMEM
    dma = pltpu.SemaphoreType.DMA
    hbm = pl.BlockSpec(memory_space=pl.ANY)
    vmem = pl.BlockSpec(memory_space=pltpu.VMEM)
    wide, thin = (T, KH * GW), (T, KH * HD)
    return pl.pallas_call(
        kernel,
        out_shape=tuple(jax.ShapeDtypeStruct(s, BF) for s in (wide, wide, thin, thin)),
        in_specs=[hbm] * 4 + [vmem] * 3,
        out_specs=(hbm,) * 4,
        scratch_shapes=[
            vm(wide, BF), vm(wide, BF), vm(thin, BF), vm(thin, BF),
            vm((T, T), BF), vm((T, T), BF), vm((T, T), BF), vm((T, T), BF),
            vm((T, 2 * KH * HD), BF), vm((T, 2 * KH * HD), BF),
            vm((KH, T, 2 * GW), BF), vm((KH, T, 2 * GW), BF),
            vm((KH, W, 2 * HD), BF), vm((W, T), F32), vm((HD, W), BF), vm((HD, W), BF),
            vm((KH, T, 2 * GW), BF), vm((KH, T, 2 * GW), BF),
            vm((KH, W, 2 * HD), BF), vm((KH, 3, 2, T, 2 * HD), BF),
            vm((KH, 3, T, 2 * HD), F32), vm((KH, 2, T, 2 * HD), BF), vm((KH, 2, T, 2 * HD), BF),
            vm((KH, T, 2 * HD), BF), vm((KH, T, 2 * HD), BF),
            vm((KH, T, 2 * GW), BF), vm(thin, BF), vm(thin, BF),
            dma((4,)), dma((KH, 2)), dma((NDP,)), dma((NDP,)),
            dma((KH, NDP)), dma((KH, NDP)), dma((KH, 3)), dma((KH, 3)),
            dma((KH, 4, 2)), dma((KH, 4, 2)), dma((KH, NDP)), dma((KH, NDP)),
            dma((KH, 4, 2)), dma((KH, 4, 2)), dma((KH, 3)), dma((KH, 3)),
            dma((KH, NDP)), dma((KH, NDP)),
        ],
        compiler_params=pltpu.CompilerParams(
            collective_id=0, has_side_effects=True, vmem_limit_bytes=60 * 2**20
        ),
    )(
        query_rows, key_rows, value_rows, grad_out,
        send_order.reshape(1, T), recv_place.reshape(1, T), doc_ids,
    )


def solution(mesh):
    rows = P(("dp", "ctx"), None)
    return jax.shard_map(
        body,
        mesh=mesh,
        in_specs=(rows,) * 4 + (P("dp", "ctx", None),) * 2 + (P("dp", None),),
        out_specs=(rows,) * 4,
        check_vma=False,
    )
```

```python
import jax
import jax.numpy as jnp
from jax import lax
from jax.experimental import pallas as pl
from jax.experimental.pallas import tpu as pltpu
from jax.sharding import PartitionSpec as P

BF, F32, I32 = jnp.bfloat16, jnp.float32, jnp.int32
MESH = pl.DeviceIdType.MESH
HD = 128
KH = 4
GS = 8
T = 128
NDP = 8
SHARE = T // NDP
NCH = 9
W = NCH * T
GW = GS * HD
SCALE = HD**-0.5
SCALE2 = SCALE * 1.4426950408889634
NEG = -1e30
NT = (((1,), (1,)), ((), ()))
NN = (((1,), (0,)), ((), ()))
Y_MSGS = ((1, 0), (2, 0), (3, 0), (1, 1), (3, 1))
Y_WAIT = tuple(m for m in Y_MSGS if m != (2, 0))
LAG = 1


def dot(a, b, dims=NN):
    return lax.dot_general(a, b, dims, preferred_element_type=F32)


def kernel(
    q_hbm, k_hbm, v_hbm, g_hbm, order_ref, place_ref, doc_ref,
    odr, zkr,
    q_in, g_in, k_in, v_in, hot, nat, nat_t,
    kvs, kvr, qgs, qgr, kv, bias, kt, vt,
    ods, dkv, y2s, yrec, x6rec, acc, xs, xrec, zks,
    in_sem, own_sem, kv_ss, kv_rs, qg_ss, qg_rs, x_ss, x_rs, y_ss, y_rs,
    od_ss, od_rs, yr_ss, yr_rs, xr_ss, xr_rs, zk_ss, zk_rs,
):
    d = lax.axis_index("dp")
    c = lax.axis_index("ctx")
    x, y = c // 4, c % 4

    def group_at(j):
        return (lax.rem(d + j, NDP), c)

    def x_at(j):
        return (d, lax.rem(x + j + 4, 4) * 4 + y)

    def y_at(j):
        return (d, x * 4 + lax.rem(y + j + 4, 4))

    bar = pltpu.get_barrier_semaphore()
    friends = [group_at(j) for j in range(1, NDP)]
    friends += [x_at(j) for j in range(1, 4)] + [y_at(j) for j in range(1, 4)]
    for f in friends:
        pl.semaphore_signal(bar, 1, device_id=f, device_id_type=MESH)

    k_cp = pltpu.make_async_copy(k_hbm, k_in, in_sem.at[0])
    v_cp = pltpu.make_async_copy(v_hbm, v_in, in_sem.at[1])
    q_cp = pltpu.make_async_copy(q_hbm, q_in, in_sem.at[2])
    g_cp = pltpu.make_async_copy(g_hbm, g_in, in_sem.at[3])
    for cp in (k_cp, v_cp, q_cp, g_cp):
        cp.start()

    rows = lax.broadcasted_iota(I32, (T, T), 0)
    hot[...] = (rows == order_ref[...]).astype(F32).T.astype(BF)
    nat32 = (rows == place_ref[...]).astype(F32)
    nat[...] = nat32.astype(BF)
    nat_t[...] = nat32.T.astype(BF)

    mine = pl.ds(pl.multiple_of(d * SHARE, SHARE), SHARE)

    def part(j):
        return pl.ds(pl.multiple_of(lax.rem(d + j, NDP) * SHARE, SHARE), SHARE)

    def rcopy(src, dst, ss, rs, to):
        return pltpu.make_async_remote_copy(
            src_ref=src, dst_ref=dst, send_sem=ss, recv_sem=rs, device_id=to, device_id_type=MESH
        )

    def kv_copy(j):
        return rcopy(kvs.at[part(j)], kvr.at[mine], kv_ss.at[j], kv_rs.at[j], group_at(j))

    def qg_copy(g, j):
        return rcopy(
            qgs.at[g, part(j)], qgr.at[g, mine], qg_ss.at[g, j], qg_rs.at[g, j], group_at(j)
        )

    def od_copy(g, j):
        return rcopy(
            ods.at[g, part(j)], odr.at[g, mine], od_ss.at[g, j], od_rs.at[g, j], group_at(j)
        )

    def zk_copy(g, j):
        return rcopy(
            zks.at[g, part(j)], zkr.at[g, mine], zk_ss.at[g, j], zk_rs.at[g, j], group_at(j)
        )

    def chunk(o):
        return pl.ds(pl.multiple_of(o * T, T), T)

    def x_copy(g, j):
        src, dst, to = ((0, 4, 1), (0, 8, 2), (2, 6, 1))[j - 1]
        return rcopy(
            kv.at[g, chunk(src)], kv.at[g, chunk(dst)], x_ss.at[g, j], x_rs.at[g, j], x_at(to)
        )

    def y_copy(g, j, b):
        turn = (y + j) // 4
        return rcopy(
            kv.at[g, chunk(4 * (turn + b))], kv.at[g, chunk(j + 4 * b)],
            y_ss.at[g, j, b], y_rs.at[g, j, b], y_at(j),
        )

    def yr_copy(g, j, b):
        src = y2s.at[g] if (j, b) == (2, 0) else dkv.at[g, chunk(j + 4 * b)]
        return rcopy(
            src, yrec.at[g, j - 1, b], yr_ss.at[g, j, b], yr_rs.at[g, j, b], y_at(-j)
        )

    def xr_copy(g, j):
        if j == 3:
            src, dst, to = dkv.at[g, chunk(6)], x6rec.at[g], 1
        else:
            src, dst, to = xs.at[g, j - 1], xrec.at[g, j - 1], j
        return rcopy(src, dst, xr_ss.at[g, j], xr_rs.at[g, j], x_at(-to))

    def own_od(g):
        return pltpu.make_async_copy(ods.at[g, mine], odr.at[g, mine], own_sem.at[g, 0])

    def own_zk(g):
        return pltpu.make_async_copy(zks.at[g, mine], zkr.at[g, mine], own_sem.at[g, 1])

    k_cp.wait()
    v_cp.wait()
    for g in range(KH):
        cols = slice(g * HD, (g + 1) * HD)
        kvs[:, 2 * g * HD : (2 * g + 1) * HD] = dot(hot[...], k_in[:, cols]).astype(BF)
        kvs[:, (2 * g + 1) * HD : (2 * g + 2) * HD] = dot(hot[...], v_in[:, cols]).astype(BF)
    kvr[mine, :] = kvs[mine, :]
    pl.semaphore_wait(bar, len(friends))
    for j in range(1, NDP):
        kv_copy(j).start()

    q_cp.wait()
    g_cp.wait()

    def send_rows(g, carry):
        cols = pl.ds(pl.multiple_of(g * GW, GW), GW)
        qgs[g, :, 0:GW] = dot(hot[...], q_in[:, cols]).astype(BF)
        qgs[g, :, GW : 2 * GW] = dot(hot[...], g_in[:, cols]).astype(BF)
        qgr[g, mine, :] = qgs[g, mine, :]
        for j in range(1, NDP):
            qg_copy(g, j).start()
        return carry

    lax.fori_loop(0, KH, send_rows, 0)

    q_pos = place_ref[...]
    own_doc = doc_ref[0:1, pl.ds(pl.multiple_of(c * T, T), T)].astype(F32).astype(BF)
    q_doc = dot(jnp.broadcast_to(own_doc, (8, T)), nat[...])[0:1]

    def mask(o, carry):
        at = lax.rem(c - o + 16, 16)
        row = doc_ref[0:1, pl.ds(pl.multiple_of(at * T, T), T)].astype(F32)
        k_doc = jnp.broadcast_to(row, (T, T)).T
        ahead = jnp.where(o == 0, rows - q_pos, 0)
        ahead = jnp.where(o <= c, ahead, 1)
        bias[chunk(o), :] = jnp.where((k_doc == q_doc) & (ahead <= 0), 0.0, NEG)
        return carry

    lax.fori_loop(0, NCH, mask, 0)

    for j in range(1, NDP):
        kv_copy(j).wait_recv()
    for g in range(KH):
        cols = slice(2 * g * HD, 2 * (g + 1) * HD)
        kv[g, 0:T, :] = dot(nat[...], kvr[:, cols]).astype(BF)
        for j in (1, 2):
            x_copy(g, j).start()

    def early(g):
        for j in (1, 2, 3):
            pl.when(y + j < 4)(y_copy(g, j, 0).start)

    def late(g):
        for j in (1, 2):
            x_copy(g, j).wait_recv()
        for j in (1, 2, 3):
            pl.when(y + j >= 4)(y_copy(g, j, 0).start)
        for j in (1, 3):
            y_copy(g, j, 1).start()

    def relay(g):
        y_copy(g, 2, 0).wait_recv()
        x_copy(g, 3).start()

    early(0)
    early(1)
    late(0)
    early(2)
    late(1)
    early(3)
    late(2)
    late(3)
    relay(0)

    def attend(g):
        for j in range(1, NDP):
            qg_copy(g, j).wait_recv()
        for j, b in Y_WAIT:
            y_copy(g, j, b).wait_recv()
        x_copy(g, 3).wait_recv()
        keys, values = kv[g, :, 0:HD], kv[g, :, HD : 2 * HD]
        kt[...] = keys.T
        vt[...] = values.T
        query = jnp.concatenate([qgr[g, :, h * HD : (h + 1) * HD] for h in range(GS)], axis=0)
        grad = jnp.concatenate(
            [qgr[g, :, GW + h * HD : GW + (h + 1) * HD] for h in range(GS)], axis=0
        )
        scores = dot(keys, query, NT) * SCALE2 + jnp.concatenate([bias[...]] * GS, axis=1)
        weights = jnp.exp2(scores - jnp.max(scores, axis=0, keepdims=True))
        probs = weights * (1.0 / jnp.sum(weights, axis=0, keepdims=True))
        probs_b = probs.astype(BF)
        out = dot(vt[...], probs_b).astype(BF)
        prob_grad = dot(values, grad, NT)
        delta = jnp.sum(out.astype(F32) * grad.T.astype(F32), axis=0, keepdims=True)
        dscore = (probs * (prob_grad - delta)).astype(BF)
        dq = (dot(kt[...], dscore) * SCALE).astype(BF)
        out, dq = out.T, dq.T
        for h in range(GS):
            ods[g, :, h * HD : (h + 1) * HD] = out[h * T : (h + 1) * T]
            ods[g, :, GW + h * HD : GW + (h + 1) * HD] = dq[h * T : (h + 1) * T]
        dkv[g, :, 0:HD] = (dot(dscore, query) * SCALE).astype(BF)
        dkv[g, :, HD : 2 * HD] = dot(probs_b, grad).astype(BF)
        xr_copy(g, 3).start()
        for j, b in Y_WAIT:
            yr_copy(g, j, b).start()
        own_od(g).start()
        for j in range(1, NDP):
            od_copy(g, j).start()

    def add_relayed(g):
        xr_copy(g, 3).wait_recv()
        there = dkv[g, 2 * T : 3 * T, :].astype(F32) + x6rec[g].astype(F32)
        y2s[g] = there.astype(BF)
        yr_copy(g, 2, 0).start()

    def add_y(g):
        for k in range(3):
            acc[g, k] = dkv[g, 4 * k * T : (4 * k + 1) * T, :].astype(F32)
        for j, b in Y_MSGS:
            turn = (y + j) // 4
            yr_copy(g, j, b).wait_recv()
            acc[g, turn + b] += yrec[g, j - 1, b].astype(F32)
        for j in (1, 2):
            xs[g, j - 1] = acc[g, j].astype(BF)
            xr_copy(g, j).start()

    def add_x(g):
        total = acc[g, 0]
        for j in (1, 2):
            xr_copy(g, j).wait_recv()
            total += xrec[g, j - 1].astype(F32)
        zks[g] = dot(nat_t[...], total.astype(BF)).astype(BF)
        own_zk(g).start()
        for j in range(1, NDP):
            zk_copy(g, j).start()

    def turn(t, carry):
        @pl.when(t < KH)
        def _():
            pl.when(t < KH - 1)(lambda: relay(t + 1))
            attend(t)

        for step, lag in ((add_relayed, LAG), (add_y, LAG + 1), (add_x, LAG + 2)):
            pl.when((t >= lag) & (t < KH + lag))(lambda step=step, lag=lag: step(t - lag))
        return carry

    lax.fori_loop(0, KH + LAG + 2, turn, 0)

    for j in range(1, NDP):
        kv_copy(j).wait_send()

    def drain(g, carry):
        for j in range(1, NDP):
            qg_copy(g, j).wait_send()
            od_copy(g, j).wait()
            zk_copy(g, j).wait()
        for j in (1, 2, 3):
            x_copy(g, j).wait_send()
            xr_copy(g, j).wait_send()
        for j, b in Y_MSGS:
            y_copy(g, j, b).wait_send()
            yr_copy(g, j, b).wait_send()
        own_od(g).wait()
        own_zk(g).wait()
        return carry

    lax.fori_loop(0, KH, drain, 0)


def home(order_ref, od_ref, zk_ref, out_ref, dq_ref, dk_ref, dv_ref):
    rows = lax.broadcasted_iota(I32, (T, T), 0)
    back = (rows == order_ref[...]).astype(F32).astype(BF)
    out_ref[...] = dot(back, od_ref[0, :, 0:GW]).astype(BF)
    dq_ref[...] = dot(back, od_ref[0, :, GW : 2 * GW]).astype(BF)
    grads = dot(back, zk_ref[0]).astype(BF)
    dk_ref[...] = grads[:, 0:HD]
    dv_ref[...] = grads[:, HD : 2 * HD]


def body(query_rows, key_rows, value_rows, grad_out, send_order, recv_place, doc_ids):
    vm = pltpu.VMEM
    dma = pltpu.SemaphoreType.DMA
    hbm = pl.BlockSpec(memory_space=pl.ANY)
    vmem = pl.BlockSpec(memory_space=pltpu.VMEM)
    wide, thin = (T, KH * GW), (T, KH * HD)
    order = send_order.reshape(1, T)
    rows_back, keys_back = pl.pallas_call(
        kernel,
        out_shape=(
            jax.ShapeDtypeStruct((KH, T, 2 * GW), BF),
            jax.ShapeDtypeStruct((KH, T, 2 * HD), BF),
        ),
        in_specs=[hbm] * 4 + [vmem] * 3,
        out_specs=(hbm,) * 2,
        scratch_shapes=[
            vm(wide, BF), vm(wide, BF), vm(thin, BF), vm(thin, BF),
            vm((T, T), BF), vm((T, T), BF), vm((T, T), BF),
            vm((T, 2 * KH * HD), BF), vm((T, 2 * KH * HD), BF),
            vm((KH, T, 2 * GW), BF), vm((KH, T, 2 * GW), BF),
            vm((KH, W, 2 * HD), BF), vm((W, T), F32), vm((HD, W), BF), vm((HD, W), BF),
            vm((KH, T, 2 * GW), BF), vm((KH, W, 2 * HD), BF),
            vm((KH, T, 2 * HD), BF), vm((KH, 3, 2, T, 2 * HD), BF), vm((KH, T, 2 * HD), BF),
            vm((KH, 3, T, 2 * HD), F32), vm((KH, 2, T, 2 * HD), BF), vm((KH, 2, T, 2 * HD), BF),
            vm((KH, T, 2 * HD), BF),
            dma((4,)), dma((KH, 2)), dma((NDP,)), dma((NDP,)),
            dma((KH, NDP)), dma((KH, NDP)), dma((KH, 4)), dma((KH, 4)),
            dma((KH, 4, 2)), dma((KH, 4, 2)), dma((KH, NDP)), dma((KH, NDP)),
            dma((KH, 4, 2)), dma((KH, 4, 2)), dma((KH, 4)), dma((KH, 4)),
            dma((KH, NDP)), dma((KH, NDP)),
        ],
        compiler_params=pltpu.CompilerParams(
            collective_id=0, has_side_effects=True, vmem_limit_bytes=56 * 2**20
        ),
    )(
        query_rows, key_rows, value_rows, grad_out,
        order, recv_place.reshape(1, T), doc_ids,
    )
    return pl.pallas_call(
        home,
        grid=(KH,),
        out_shape=tuple(jax.ShapeDtypeStruct(s, BF) for s in (wide, wide, thin, thin)),
        in_specs=[
            pl.BlockSpec((1, T), lambda g: (0, 0)),
            pl.BlockSpec((1, T, 2 * GW), lambda g: (g, 0, 0)),
            pl.BlockSpec((1, T, 2 * HD), lambda g: (g, 0, 0)),
        ],
        out_specs=tuple(
            pl.BlockSpec((T, n), lambda g: (0, g)) for n in (GW, GW, HD, HD)
        ),
    )(order, rows_back, keys_back)


def solution(mesh):
    rows = P(("dp", "ctx"), None)
    return jax.shard_map(
        body,
        mesh=mesh,
        in_specs=(rows,) * 4 + (P("dp", "ctx", None),) * 2 + (P("dp", None),),
        out_specs=(rows,) * 4,
        check_vma=False,
    )
```

```python
import jax
import jax.numpy as jnp
from jax import lax
from jax.experimental import pallas as pl
from jax.experimental.pallas import tpu as pltpu
from jax.sharding import PartitionSpec as P

BF, F32, I32 = jnp.bfloat16, jnp.float32, jnp.int32
MESH = pl.DeviceIdType.MESH
HD = 128
KH = 4
GS = 8
T = 128
NDP = 8
SHARE = T // NDP
NCH = 9
W = NCH * T
GW = GS * HD
SCALE = HD**-0.5
SCALE2 = SCALE * 1.4426950408889634
NEG = -1e30
NT = (((1,), (1,)), ((), ()))
NN = (((1,), (0,)), ((), ()))
Y_MSGS = ((1, 0), (2, 0), (3, 0), (1, 1), (3, 1))
Y_WAIT = tuple(m for m in Y_MSGS if m != (2, 0))
LAG = 1


def dot(a, b, dims=NN):
    return lax.dot_general(a, b, dims, preferred_element_type=F32)


def kernel(
    q_hbm, k_hbm, v_hbm, g_hbm, order_hbm, place_hbm, doc_hbm,
    odr, zkr,
    q_in, g_in, k_in, v_in, hot, nat, nat_t,
    kvs, kvr, qgs, qgr, kv, bias, kt, vt,
    ods, dkv, y2s, yrec, x6rec, acc, xs, xrec, zks,
    order_ref, place_ref, doc_ref, in_sem, own_sem, sent, kv_rs, qg_rs, x_rs, x6_rs, y_rs, y2_rs,
    od_rs, yr_rs, xr_rs, xr6_rs, zk_rs,
):
    d = lax.axis_index("dp")
    c = lax.axis_index("ctx")
    x, y = c // 4, c % 4

    def group_at(j):
        return (lax.rem(d + j, NDP), c)

    def x_at(j):
        return (d, lax.rem(x + j + 4, 4) * 4 + y)

    def y_at(j):
        return (d, x * 4 + lax.rem(y + j + 4, 4))

    bar = pltpu.get_barrier_semaphore()
    friends = [group_at(j) for j in range(1, NDP)]
    friends += [x_at(j) for j in range(1, 4)] + [y_at(j) for j in range(1, 4)]
    for f in friends:
        pl.semaphore_signal(bar, 1, device_id=f, device_id_type=MESH)

    pairs = (
        (order_hbm, order_ref), (k_hbm, k_in), (v_hbm, v_in), (place_hbm, place_ref),
        (doc_hbm, doc_ref), (q_hbm, q_in), (g_hbm, g_in),
    )
    arrivals = [pltpu.make_async_copy(a, b, in_sem.at[n]) for n, (a, b) in enumerate(pairs)]
    for cp in arrivals:
        cp.start()

    rows = lax.broadcasted_iota(I32, (T, T), 0)
    arrivals[0].wait()
    hot[...] = (rows == order_ref[...]).astype(F32).T.astype(BF)
    mine = pl.ds(pl.multiple_of(d * SHARE, SHARE), SHARE)

    def part(j):
        return pl.ds(pl.multiple_of(lax.rem(d + j, NDP) * SHARE, SHARE), SHARE)

    def rcopy(src, dst, ss, rs, to):
        return pltpu.make_async_remote_copy(
            src_ref=src, dst_ref=dst, send_sem=ss, recv_sem=rs, device_id=to, device_id_type=MESH
        )

    def a2a(src, dst, sem, rs, j):
        return rcopy(src.at[part(j)], dst.at[mine], sent.at[sem], rs, group_at(j))

    def kv_copy(j):
        return a2a(kvs, kvr, 0, kv_rs.at[0], j)

    def qg_copy(g, j):
        return a2a(qgs.at[g], qgr.at[g], 1, qg_rs.at[g], j)

    def od_copy(g, j):
        return a2a(ods.at[g], odr.at[g], 2, od_rs.at[0], j)

    def zk_copy(g, j):
        return a2a(zks.at[g], zkr.at[g], 3, zk_rs.at[0], j)

    def landed(ref, rs):
        rcopy(ref, ref, sent.at[0], rs, group_at(1)).wait_recv()

    def left(ref, sem):
        rcopy(ref, ref, sent.at[sem], kv_rs.at[0], group_at(1)).wait_send()

    def chunk(o):
        return pl.ds(pl.multiple_of(o * T, T), T)

    def x_copy(g, j):
        src, dst, to = ((0, 4, 1), (0, 8, 2), (2, 6, 1))[j - 1]
        rs = (x6_rs if j == 3 else x_rs).at[g]
        return rcopy(kv.at[g, chunk(src)], kv.at[g, chunk(dst)], sent.at[4], rs, x_at(to))

    def y_copy(g, j, b):
        src = 4 * ((y + j) // 4 + b)
        rs = (y2_rs if (j, b) == (2, 0) else y_rs).at[g]
        return rcopy(
            kv.at[g, chunk(src)], kv.at[g, chunk(j + 4 * b)], sent.at[5], rs, y_at(j)
        )

    def yr_copy(g, j, b):
        src = y2s.at[g] if (j, b) == (2, 0) else dkv.at[g, chunk(j + 4 * b)]
        return rcopy(src, yrec.at[g, chunk(Y_MSGS.index((j, b)))], sent.at[6], yr_rs.at[g], y_at(-j))

    def xr_copy(g, j):
        if j == 3:
            return rcopy(dkv.at[g, chunk(6)], x6rec.at[g], sent.at[7], xr6_rs.at[g], x_at(-1))
        return rcopy(
            xs.at[g, chunk(j - 1)], xrec.at[g, chunk(j - 1)], sent.at[7], xr_rs.at[g], x_at(-j)
        )

    def own_od():
        return pltpu.make_async_copy(ods.at[:, mine], odr.at[:, mine], own_sem.at[0])

    def own_zk():
        return pltpu.make_async_copy(zks.at[:, mine], zkr.at[:, mine], own_sem.at[1])

    arrivals[1].wait()
    arrivals[2].wait()
    for g in range(KH):
        cols = slice(g * HD, (g + 1) * HD)
        kvs[:, 2 * g * HD : (2 * g + 1) * HD] = dot(hot[...], k_in[:, cols]).astype(BF)
        kvs[:, (2 * g + 1) * HD : (2 * g + 2) * HD] = dot(hot[...], v_in[:, cols]).astype(BF)
    kvr[mine, :] = kvs[mine, :]
    pl.semaphore_wait(bar, len(friends))
    for j in range(1, NDP):
        kv_copy(j).start()

    arrivals[5].wait()
    arrivals[6].wait()

    def send_rows(g, carry):
        cols = pl.ds(pl.multiple_of(g * GW, GW), GW)
        qgs[g, :, 0:GW] = dot(hot[...], q_in[:, cols]).astype(BF)
        qgs[g, :, GW : 2 * GW] = dot(hot[...], g_in[:, cols]).astype(BF)
        qgr[g, mine, :] = qgs[g, mine, :]
        for j in range(1, NDP):
            qg_copy(g, j).start()
        return carry

    lax.fori_loop(0, KH, send_rows, 0)

    arrivals[3].wait()
    arrivals[4].wait()
    nat32 = (rows == place_ref[...]).astype(F32)
    nat[...] = nat32.astype(BF)
    nat_t[...] = nat32.T.astype(BF)
    q_pos = place_ref[...]
    own_doc = doc_ref[0:1, pl.ds(pl.multiple_of(c * T, T), T)].astype(F32).astype(BF)
    q_doc = dot(jnp.broadcast_to(own_doc, (8, T)), nat[...])[0:1]

    def mask(o, carry):
        at = lax.rem(c - o + 16, 16)
        row = doc_ref[0:1, pl.ds(pl.multiple_of(at * T, T), T)].astype(F32)
        k_doc = jnp.broadcast_to(row, (T, T)).T
        ahead = jnp.where(o == 0, rows - q_pos, 0)
        ahead = jnp.where(o <= c, ahead, 1)
        bias[chunk(o), :] = jnp.where((k_doc == q_doc) & (ahead <= 0), 0.0, NEG)
        return carry

    lax.fori_loop(0, NCH, mask, 0)

    others = pl.ds(0, T - SHARE)
    landed(kvr.at[others], kv_rs.at[0])
    for g in range(KH):
        cols = slice(2 * g * HD, 2 * (g + 1) * HD)
        kv[g, 0:T, :] = dot(nat[...], kvr[:, cols]).astype(BF)
        for j in (1, 2):
            x_copy(g, j).start()

    def early(g):
        for j in (1, 2, 3):
            pl.when(y + j < 4)(y_copy(g, j, 0).start)

    def late(g):
        landed(kv.at[g, pl.ds(0, 2 * T)], x_rs.at[g])
        for j in (1, 2, 3):
            pl.when(y + j >= 4)(y_copy(g, j, 0).start)
        for j in (1, 3):
            y_copy(g, j, 1).start()

    def relay(g):
        landed(kv.at[g, pl.ds(0, T)], y2_rs.at[g])
        x_copy(g, 3).start()

    early(0)
    early(1)
    late(0)
    early(2)
    late(1)
    early(3)
    late(2)
    late(3)
    relay(0)

    def attend(g):
        landed(qgr.at[g, others], qg_rs.at[g])
        landed(kv.at[g, pl.ds(0, 4 * T)], y_rs.at[g])
        landed(kv.at[g, pl.ds(0, T)], x6_rs.at[g])
        keys, values = kv[g, :, 0:HD], kv[g, :, HD : 2 * HD]
        kt[...] = keys.T
        vt[...] = values.T
        query = jnp.concatenate([qgr[g, :, h * HD : (h + 1) * HD] for h in range(GS)], axis=0)
        grad = jnp.concatenate(
            [qgr[g, :, GW + h * HD : GW + (h + 1) * HD] for h in range(GS)], axis=0
        )
        scores = dot(keys, query, NT) * SCALE2 + jnp.concatenate([bias[...]] * GS, axis=1)
        weights = jnp.exp2(scores - jnp.max(scores, axis=0, keepdims=True))
        probs = weights * (1.0 / jnp.sum(weights, axis=0, keepdims=True))
        probs_b = probs.astype(BF)
        out = dot(vt[...], probs_b).astype(BF)
        prob_grad = dot(values, grad, NT)
        delta = jnp.sum(out.astype(F32) * grad.T.astype(F32), axis=0, keepdims=True)
        dscore = (probs * (prob_grad - delta)).astype(BF)
        dq = (dot(kt[...], dscore) * SCALE).astype(BF)
        out, dq = out.T, dq.T
        for h in range(GS):
            ods[g, :, h * HD : (h + 1) * HD] = out[h * T : (h + 1) * T]
            ods[g, :, GW + h * HD : GW + (h + 1) * HD] = dq[h * T : (h + 1) * T]
        dkv[g, :, 0:HD] = (dot(dscore, query) * SCALE).astype(BF)
        dkv[g, :, HD : 2 * HD] = dot(probs_b, grad).astype(BF)
        xr_copy(g, 3).start()
        for j, b in Y_WAIT:
            yr_copy(g, j, b).start()
        for j in range(1, NDP):
            od_copy(g, j).start()

    def add_relayed(g):
        landed(x6rec.at[g], xr6_rs.at[g])
        there = dkv[g, 2 * T : 3 * T, :].astype(F32) + x6rec[g].astype(F32)
        y2s[g] = there.astype(BF)
        yr_copy(g, 2, 0).start()

    def add_y(g):
        for k in range(3):
            acc[g, k] = dkv[g, 4 * k * T : (4 * k + 1) * T, :].astype(F32)
        landed(yrec.at[g], yr_rs.at[g])
        for n, (j, b) in enumerate(Y_MSGS):
            acc[g, (y + j) // 4 + b] += yrec[g, n * T : (n + 1) * T, :].astype(F32)
        for j in (1, 2):
            xs[g, (j - 1) * T : j * T, :] = acc[g, j].astype(BF)
            xr_copy(g, j).start()

    def add_x(g):
        landed(xrec.at[g], xr_rs.at[g])
        total = acc[g, 0]
        for j in (1, 2):
            total += xrec[g, (j - 1) * T : j * T, :].astype(F32)
        zks[g] = dot(nat_t[...], total.astype(BF)).astype(BF)
        for j in range(1, NDP):
            zk_copy(g, j).start()

    def turn(t, carry):
        @pl.when(t < KH)
        def _():
            pl.when(t < KH - 1)(lambda: relay(t + 1))
            attend(t)

        for step, lag in ((add_relayed, LAG), (add_y, LAG + 1), (add_x, LAG + 2)):
            pl.when((t >= lag) & (t < KH + lag))(lambda step=step, lag=lag: step(t - lag))
        return carry

    lax.fori_loop(0, KH + LAG + 2, turn, 0)

    own_od().start()
    own_zk().start()
    left(kvs.at[others], 0)
    left(qgs.at[:, others], 1)
    left(ods.at[:, others], 2)
    left(zks.at[:, others], 3)
    left(kv.at[:, pl.ds(0, 3 * T)], 4)
    left(yrec, 5)
    left(yrec, 6)
    left(kv.at[:, pl.ds(0, 3 * T)], 7)
    landed(odr.at[:, others], od_rs.at[0])
    landed(zkr.at[:, others], zk_rs.at[0])
    own_od().wait()
    own_zk().wait()


def home(order_ref, od_hbm, zk_hbm, out_hbm, dq_hbm, dk_hbm, dv_hbm, od, zk, res, gk, gv, sem):
    def come(g):
        return pltpu.make_async_copy(od_hbm.at[g], od.at[g], sem.at[g])

    def leave(g):
        cols = pl.ds(g * GW, GW)
        return (
            pltpu.make_async_copy(res.at[g, :, pl.ds(0, GW)], out_hbm.at[:, cols], sem.at[KH + g]),
            pltpu.make_async_copy(res.at[g, :, pl.ds(GW, GW)], dq_hbm.at[:, cols], sem.at[2 * KH + g]),
        )

    zk_cp = pltpu.make_async_copy(zk_hbm, zk, sem.at[3 * KH])
    for g in range(KH):
        come(g).start()
    zk_cp.start()
    rows = lax.broadcasted_iota(I32, (T, T), 0)
    back = (rows == order_ref[...]).astype(F32).astype(BF)
    for g in range(KH):
        come(g).wait()
        res[g] = dot(back, od[g]).astype(BF)
        for cp in leave(g):
            cp.start()
    zk_cp.wait()
    for g in range(KH):
        grads = dot(back, zk[g]).astype(BF)
        gk[:, g * HD : (g + 1) * HD] = grads[:, 0:HD]
        gv[:, g * HD : (g + 1) * HD] = grads[:, HD : 2 * HD]
    ends = [pltpu.make_async_copy(gk, dk_hbm, sem.at[3 * KH + 1])]
    ends.append(pltpu.make_async_copy(gv, dv_hbm, sem.at[3 * KH + 2]))
    for cp in ends:
        cp.start()
    for g in range(KH):
        for cp in leave(g):
            cp.wait()
    for cp in ends:
        cp.wait()


def body(query_rows, key_rows, value_rows, grad_out, send_order, recv_place, doc_ids):
    vm = pltpu.VMEM
    dma = pltpu.SemaphoreType.DMA
    hbm = pl.BlockSpec(memory_space=pl.ANY)
    vmem = pl.BlockSpec(memory_space=pltpu.VMEM)
    wide, thin = (T, KH * GW), (T, KH * HD)
    order = send_order.reshape(1, T)
    rows_back, keys_back = pl.pallas_call(
        kernel,
        out_shape=(
            jax.ShapeDtypeStruct((KH, T, 2 * GW), BF),
            jax.ShapeDtypeStruct((KH, T, 2 * HD), BF),
        ),
        in_specs=[hbm] * 7,
        out_specs=(hbm,) * 2,
        scratch_shapes=[
            vm(wide, BF), vm(wide, BF), vm(thin, BF), vm(thin, BF),
            vm((T, T), BF), vm((T, T), BF), vm((T, T), BF),
            vm((T, 2 * KH * HD), BF), vm((T, 2 * KH * HD), BF),
            vm((KH, T, 2 * GW), BF), vm((KH, T, 2 * GW), BF),
            vm((KH, W, 2 * HD), BF), vm((W, T), F32), vm((HD, W), BF), vm((HD, W), BF),
            vm((KH, T, 2 * GW), BF), vm((KH, W, 2 * HD), BF),
            vm((KH, T, 2 * HD), BF), vm((KH, 5 * T, 2 * HD), BF), vm((KH, T, 2 * HD), BF),
            vm((KH, 3, T, 2 * HD), F32), vm((KH, 2 * T, 2 * HD), BF), vm((KH, 2 * T, 2 * HD), BF),
            vm((KH, T, 2 * HD), BF),
            vm((1, T), I32), vm((1, T), I32), vm(doc_ids.shape, I32), dma((7,)), dma((2,)),
            dma((8,)), dma((1,)), dma((KH,)), dma((KH,)), dma((KH,)), dma((KH,)), dma((KH,)),
            dma((1,)), dma((KH,)), dma((KH,)), dma((KH,)), dma((1,)),
        ],
        compiler_params=pltpu.CompilerParams(
            collective_id=0, has_side_effects=True, vmem_limit_bytes=56 * 2**20
        ),
    )(
        query_rows, key_rows, value_rows, grad_out,
        order, recv_place.reshape(1, T), doc_ids,
    )
    return pl.pallas_call(
        home,
        out_shape=tuple(jax.ShapeDtypeStruct(s, BF) for s in (wide, wide, thin, thin)),
        in_specs=[vmem, hbm, hbm],
        out_specs=(hbm,) * 4,
        scratch_shapes=[
            vm((KH, T, 2 * GW), BF), vm((KH, T, 2 * HD), BF), vm((KH, T, 2 * GW), BF),
            vm(thin, BF), vm(thin, BF), dma((3 * KH + 3,)),
        ],
        compiler_params=pltpu.CompilerParams(vmem_limit_bytes=16 * 2**20),
    )(order, rows_back, keys_back)


def solution(mesh):
    rows = P(("dp", "ctx"), None)
    return jax.shard_map(
        body,
        mesh=mesh,
        in_specs=(rows,) * 4 + (P("dp", "ctx", None),) * 2 + (P("dp", None),),
        out_specs=(rows,) * 4,
        check_vma=False,
    )
```

```python
import jax
import jax.numpy as jnp
from jax import lax
from jax.experimental import pallas as pl
from jax.experimental.pallas import tpu as pltpu
from jax.sharding import PartitionSpec as P

BF, F32, I32 = jnp.bfloat16, jnp.float32, jnp.int32
MESH = pl.DeviceIdType.MESH
HD = 128
KH = 4
GS = 8
T = 128
NDP = 8
SHARE = T // NDP
NCH = 9
W = NCH * T
GW = GS * HD
SCALE = HD**-0.5
SCALE2 = SCALE * 1.4426950408889634
NEG = -1e30
NT = (((1,), (1,)), ((), ()))
NN = (((1,), (0,)), ((), ()))
Y_MSGS = ((1, 0), (2, 0), (3, 0), (1, 1), (3, 1))
LAG = 1
KEYS_DIRECT = ()
GRADS_DIRECT = (3,)


def dot(a, b, dims=NN):
    return lax.dot_general(a, b, dims, preferred_element_type=F32)


def kernel(
    q_hbm, k_hbm, v_hbm, g_hbm, order_hbm, place_hbm, doc_hbm,
    odr, zkr,
    q_in, g_in, k_in, v_in, hot, nat, nat_t,
    kvs, kvr, qgs, qgr, kv, bias, kt, vt,
    ods, dkv, y2s, yrec, x6rec, acc, xs, xrec, zks,
    probs, probs_b, dscore, delta, order_ref, place_ref, doc_ref, in_sem, own_sem, sent, kv_rs, qg_rs, x_rs, x6_rs, y_rs, y2_rs,
    od_rs, yr_rs, xr_rs, xr6_rs, zk_rs,
):
    d = lax.axis_index("dp")
    c = lax.axis_index("ctx")
    x, y = c // 4, c % 4

    def group_at(j):
        return (lax.rem(d + j, NDP), c)

    def x_at(j):
        return (d, lax.rem(x + j + 4, 4) * 4 + y)

    def y_at(j):
        return (d, x * 4 + lax.rem(y + j + 4, 4))

    bar = pltpu.get_barrier_semaphore()
    friends = [group_at(j) for j in range(1, NDP)]
    friends += [x_at(j) for j in range(1, 4)] + [y_at(j) for j in range(1, 4)]
    for f in friends:
        pl.semaphore_signal(bar, 1, device_id=f, device_id_type=MESH)

    pairs = (
        (order_hbm, order_ref), (k_hbm, k_in), (v_hbm, v_in), (place_hbm, place_ref),
        (doc_hbm, doc_ref), (q_hbm, q_in), (g_hbm, g_in),
    )
    arrivals = [pltpu.make_async_copy(a, b, in_sem.at[n]) for n, (a, b) in enumerate(pairs)]
    for cp in arrivals:
        cp.start()

    rows = lax.broadcasted_iota(I32, (T, T), 0)
    arrivals[0].wait()
    hot[...] = (rows == order_ref[...]).astype(F32).T.astype(BF)
    mine = pl.ds(pl.multiple_of(d * SHARE, SHARE), SHARE)

    def part(j):
        return pl.ds(pl.multiple_of(lax.rem(d + j, NDP) * SHARE, SHARE), SHARE)

    def rcopy(src, dst, ss, rs, to):
        return pltpu.make_async_remote_copy(
            src_ref=src, dst_ref=dst, send_sem=ss, recv_sem=rs, device_id=to, device_id_type=MESH
        )

    def a2a(src, dst, sem, rs, j):
        return rcopy(src.at[part(j)], dst.at[mine], sent.at[sem], rs, group_at(j))

    def kv_copy(g, j):
        return a2a(kvs.at[g], kvr.at[g], 0, kv_rs.at[g], j)

    def qg_copy(g, j):
        return a2a(qgs.at[g], qgr.at[g], 1, qg_rs.at[g], j)

    def od_copy(g, j):
        return a2a(ods.at[g], odr.at[g], 2, od_rs.at[0], j)

    def zk_copy(g, j):
        return a2a(zks.at[g], zkr.at[g], 3, zk_rs.at[0], j)

    def landed(ref, rs):
        rcopy(ref, ref, sent.at[0], rs, group_at(1)).wait_recv()

    def left(ref, sem):
        rcopy(ref, ref, sent.at[sem], kv_rs.at[0], group_at(1)).wait_send()

    def chunk(o):
        return pl.ds(pl.multiple_of(o * T, T), T)

    def x_copy(g, j):
        return rcopy(
            kv.at[g, chunk(0)], kv.at[g, chunk(4 * j)], sent.at[4], x_rs.at[g], x_at(j)
        )

    def x_relay(g):
        return rcopy(kv.at[g, chunk(2)], kv.at[g, chunk(6)], sent.at[8], x6_rs.at[g], x_at(1))

    def y_direct(g):
        src = 4 * ((y + 2) // 4 + 1)
        return rcopy(kv.at[g, chunk(src)], kv.at[g, chunk(6)], sent.at[8], x6_rs.at[g], y_at(2))

    def yr_direct(g, j):
        if j == 6:
            return rcopy(dkv.at[g, chunk(6)], x6rec.at[g], sent.at[9], xr6_rs.at[g], y_at(-2))
        at = chunk(Y_MSGS.index((2, 0)))
        return rcopy(
            dkv.at[g, chunk(2)], yrec.at[g, at], sent.at[6], yr_rs.at[g], y_at(-2)
        )

    def grads_direct(g):
        flag = g < 0
        for n in GRADS_DIRECT:
            flag |= g == n
        return flag

    def y_copy(g, j, b):
        src = 4 * ((y + j) // 4 + b)
        rs = (y2_rs if (j, b) == (2, 0) else y_rs).at[g]
        return rcopy(kv.at[g, chunk(src)], kv.at[g, chunk(j + 4 * b)], sent.at[5], rs, y_at(j))

    def yr_copy(g, j, b):
        src = y2s.at[g] if (j, b) == (2, 0) else dkv.at[g, chunk(j + 4 * b)]
        return rcopy(src, yrec.at[g, chunk(Y_MSGS.index((j, b)))], sent.at[6], yr_rs.at[g], y_at(-j))

    def xr_relay(g):
        return rcopy(dkv.at[g, chunk(6)], x6rec.at[g], sent.at[9], xr6_rs.at[g], x_at(-1))

    def xr_copy(g, j):
        return rcopy(
            xs.at[g, chunk(j - 1)], xrec.at[g, chunk(j - 1)], sent.at[7], xr_rs.at[g], x_at(-j)
        )

    def own_od():
        return pltpu.make_async_copy(ods.at[:, mine], odr.at[:, mine], own_sem.at[0])

    def own_zk():
        return pltpu.make_async_copy(zks.at[:, mine], zkr.at[:, mine], own_sem.at[1])

    arrivals[1].wait()
    arrivals[2].wait()
    for g in range(KH):
        cols = slice(g * HD, (g + 1) * HD)
        kvs[g, :, 0:HD] = dot(hot[...], k_in[:, cols]).astype(BF)
        kvs[g, :, HD : 2 * HD] = dot(hot[...], v_in[:, cols]).astype(BF)
    kvr[:, mine, :] = kvs[:, mine, :]
    pl.semaphore_wait(bar, len(friends))
    for g in range(KH):
        for j in range(1, NDP):
            kv_copy(g, j).start()

    arrivals[5].wait()
    arrivals[6].wait()

    def send_rows(g, carry):
        cols = pl.ds(pl.multiple_of(g * GW, GW), GW)
        qgs[g, :, 0:GW] = dot(hot[...], q_in[:, cols]).astype(BF)
        qgs[g, :, GW : 2 * GW] = dot(hot[...], g_in[:, cols]).astype(BF)
        qgr[g, mine, :] = qgs[g, mine, :]
        for j in range(1, NDP):
            qg_copy(g, j).start()
        return carry

    lax.fori_loop(0, KH, send_rows, 0)

    arrivals[3].wait()
    arrivals[4].wait()
    nat32 = (rows == place_ref[...]).astype(F32)
    nat[...] = nat32.astype(BF)
    nat_t[...] = nat32.T.astype(BF)
    q_pos = place_ref[...]
    own_doc = doc_ref[0:1, pl.ds(pl.multiple_of(c * T, T), T)].astype(F32).astype(BF)
    q_doc = dot(jnp.broadcast_to(own_doc, (8, T)), nat[...])[0:1]

    def mask(o, carry):
        at = lax.rem(c - o + 16, 16)
        row = doc_ref[0:1, pl.ds(pl.multiple_of(at * T, T), T)].astype(F32)
        k_doc = jnp.broadcast_to(row, (T, T)).T
        ahead = jnp.where(o == 0, rows - q_pos, 0)
        ahead = jnp.where(o <= c, ahead, 1)
        bias[chunk(o), :] = jnp.where((k_doc == q_doc) & (ahead <= 0), 0.0, NEG)
        return carry

    lax.fori_loop(0, NCH, mask, 0)

    others = pl.ds(0, T - SHARE)
    def own(g):
        landed(kvr.at[g, others], kv_rs.at[g])
        kv[g, 0:T, :] = dot(nat[...], kvr[g]).astype(BF)
        for j in (1, 2):
            x_copy(g, j).start()

    def early(g):
        for j in (2, 1, 3):
            pl.when(y + j < 4)(y_copy(g, j, 0).start)

    def late(g):
        landed(kv.at[g, pl.ds(0, 2 * T)], x_rs.at[g])
        for j in (2, 1, 3):
            pl.when(y + j >= 4)(y_copy(g, j, 0).start)
        for j in (1, 3):
            y_copy(g, j, 1).start()
        if g in KEYS_DIRECT:
            y_direct(g).start()

    def relay(g):
        landed(kv.at[g, pl.ds(0, T)], y2_rs.at[g])
        if g not in KEYS_DIRECT:
            x_relay(g).start()

    own(0)
    early(0)
    own(1)
    late(0)
    early(1)
    relay(0)
    late(1)
    own(2)
    early(2)
    relay(1)

    def stacked(g, at):
        return jnp.concatenate(
            [qgr[g, :, at + h * HD : at + (h + 1) * HD] for h in range(GS)], axis=0
        )

    def spread(g, at, rows):
        for h in range(GS):
            ods[g, :, at + h * HD : at + (h + 1) * HD] = rows[h * T : (h + 1) * T]

    def attend(g):
        landed(qgr.at[g, others], qg_rs.at[g])
        landed(kv.at[g, pl.ds(0, 4 * T)], y_rs.at[g])
        landed(kv.at[g, pl.ds(0, T)], x6_rs.at[g])
        kt[...] = kv[g, :, 0:HD].T
        vt[...] = kv[g, :, HD : 2 * HD].T
        scores = dot(kv[g, :, 0:HD], stacked(g, 0), NT) * SCALE2
        scores += jnp.concatenate([bias[...]] * GS, axis=1)
        weights = jnp.exp2(scores - jnp.max(scores, axis=0, keepdims=True))
        held = weights * (1.0 / jnp.sum(weights, axis=0, keepdims=True))
        probs[...] = held
        probs_b[...] = held.astype(BF)
        out = dot(vt[...], probs_b[...]).astype(BF)
        delta[...] = jnp.sum(
            out.astype(F32) * stacked(g, GW).T.astype(F32), axis=0, keepdims=True
        )
        spread(g, 0, out.T)

    def key_grads(g):
        prob_grad = dot(kv[g, :, HD : 2 * HD], stacked(g, GW), NT)
        dscore[...] = (probs[...] * (prob_grad - delta[...])).astype(BF)
        dkv[g, :, 0:HD] = (dot(dscore[...], stacked(g, 0)) * SCALE).astype(BF)
        dkv[g, :, HD : 2 * HD] = dot(probs_b[...], stacked(g, GW)).astype(BF)
        pl.when(jnp.logical_not(grads_direct(g)))(xr_relay(g).start)

        @pl.when(grads_direct(g))
        def _():
            yr_direct(g, 2).start()
            yr_direct(g, 6).start()

        for j, b in ((1, 0), (3, 0), (1, 1), (3, 1)):
            yr_copy(g, j, b).start()

    def query_grads(g):
        spread(g, GW, (dot(kt[...], dscore[...]) * SCALE).astype(BF).T)
        for j in range(1, NDP):
            od_copy(g, j).start()

    def add_relayed(g):
        @pl.when(jnp.logical_not(grads_direct(g)))
        def _():
            landed(x6rec.at[g], xr6_rs.at[g])
            there = dkv[g, 2 * T : 3 * T, :].astype(F32) + x6rec[g].astype(F32)
            y2s[g] = there.astype(BF)
            yr_copy(g, 2, 0).start()

    def add_y(g):
        for k in range(3):
            acc[g, k] = dkv[g, 4 * k * T : (4 * k + 1) * T, :].astype(F32)
        landed(yrec.at[g], yr_rs.at[g])
        for n, (j, b) in enumerate(Y_MSGS):
            acc[g, (y + j) // 4 + b] += yrec[g, n * T : (n + 1) * T, :].astype(F32)

        @pl.when(grads_direct(g))
        def _():
            landed(x6rec.at[g], xr6_rs.at[g])
            acc[g, (y + 2) // 4 + 1] += x6rec[g].astype(F32)

        for j in (1, 2):
            xs[g, (j - 1) * T : j * T, :] = acc[g, j].astype(BF)
            xr_copy(g, j).start()

    def add_x(g):
        landed(xrec.at[g], xr_rs.at[g])
        total = acc[g, 0]
        for j in (1, 2):
            total += xrec[g, (j - 1) * T : j * T, :].astype(F32)
        zks[g] = dot(nat_t[...], total.astype(BF)).astype(BF)
        for j in range(1, NDP):
            zk_copy(g, j).start()

    def turn(t, carry):
        @pl.when(t < KH)
        def _():
            attend(t)

            @pl.when(t == 0)
            def _():
                late(2)
                own(3)
                early(3)

            @pl.when(t == 1)
            def _():
                late(3)
                relay(2)

            pl.when(t == 2)(lambda: relay(3))
            key_grads(t)

        for step, lag in ((add_relayed, LAG), (add_y, LAG + 1), (add_x, LAG + 2)):
            pl.when((t >= lag) & (t < KH + lag))(lambda step=step, lag=lag: step(t - lag))
        pl.when(t < KH)(lambda: query_grads(t))
        return carry

    lax.fori_loop(0, KH + LAG + 2, turn, 0)

    own_od().start()
    own_zk().start()
    left(kvs.at[:, others], 0)
    left(qgs.at[:, others], 1)
    left(ods.at[:, others], 2)
    left(zks.at[:, others], 3)
    left(kv.at[:, pl.ds(0, 2 * T)], 4)
    left(kv.at[:, pl.ds(0, T)], 8)
    left(kv.at[:, pl.ds(0, T)], 9)
    left(yrec, 5)
    left(yrec, 6)
    left(kv.at[:, pl.ds(0, 2 * T)], 7)
    landed(odr.at[:, others], od_rs.at[0])
    landed(zkr.at[:, others], zk_rs.at[0])
    own_od().wait()
    own_zk().wait()


def home(order_ref, od, zk, out_hbm, dq_hbm, dk_hbm, dv_hbm, res, gk, gv, sem):
    def leave(g):
        cols = pl.ds(g * GW, GW)
        return (
            pltpu.make_async_copy(res.at[g, :, pl.ds(0, GW)], out_hbm.at[:, cols], sem.at[g]),
            pltpu.make_async_copy(res.at[g, :, pl.ds(GW, GW)], dq_hbm.at[:, cols], sem.at[KH + g]),
        )

    rows = lax.broadcasted_iota(I32, (T, T), 0)
    back = (rows == order_ref[...]).astype(F32).astype(BF)
    for g in range(KH):
        res[g] = dot(back, od[g]).astype(BF)
        for cp in leave(g):
            cp.start()
    for g in range(KH):
        grads = dot(back, zk[g]).astype(BF)
        gk[:, g * HD : (g + 1) * HD] = grads[:, 0:HD]
        gv[:, g * HD : (g + 1) * HD] = grads[:, HD : 2 * HD]
    ends = [pltpu.make_async_copy(gk, dk_hbm, sem.at[2 * KH])]
    ends.append(pltpu.make_async_copy(gv, dv_hbm, sem.at[2 * KH + 1]))
    for cp in ends:
        cp.start()
    for g in range(KH):
        for cp in leave(g):
            cp.wait()
    for cp in ends:
        cp.wait()


def body(query_rows, key_rows, value_rows, grad_out, send_order, recv_place, doc_ids):
    vm = pltpu.VMEM
    dma = pltpu.SemaphoreType.DMA
    hbm = pl.BlockSpec(memory_space=pl.ANY)
    vmem = pl.BlockSpec(memory_space=pltpu.VMEM)
    wide, thin = (T, KH * GW), (T, KH * HD)
    order = send_order.reshape(1, T)
    rows_back, keys_back = pl.pallas_call(
        kernel,
        out_shape=(
            jax.ShapeDtypeStruct((KH, T, 2 * GW), BF),
            jax.ShapeDtypeStruct((KH, T, 2 * HD), BF),
        ),
        in_specs=[hbm] * 7,
        out_specs=(hbm,) * 2,
        scratch_shapes=[
            vm(wide, BF), vm(wide, BF), vm(thin, BF), vm(thin, BF),
            vm((T, T), BF), vm((T, T), BF), vm((T, T), BF),
            vm((KH, T, 2 * HD), BF), vm((KH, T, 2 * HD), BF),
            vm((KH, T, 2 * GW), BF), vm((KH, T, 2 * GW), BF),
            vm((KH, W, 2 * HD), BF), vm((W, T), F32), vm((HD, W), BF), vm((HD, W), BF),
            vm((KH, T, 2 * GW), BF), vm((KH, W, 2 * HD), BF),
            vm((KH, T, 2 * HD), BF), vm((KH, 5 * T, 2 * HD), BF), vm((KH, T, 2 * HD), BF),
            vm((KH, 3, T, 2 * HD), F32), vm((KH, 2 * T, 2 * HD), BF), vm((KH, 2 * T, 2 * HD), BF),
            vm((KH, T, 2 * HD), BF),
            vm((W, GW), F32), vm((W, GW), BF), vm((W, GW), BF), vm((1, GW), F32),
            vm((1, T), I32), vm((1, T), I32), vm(doc_ids.shape, I32), dma((7,)), dma((2,)),
            dma((10,)), dma((KH,)), dma((KH,)), dma((KH,)), dma((KH,)), dma((KH,)), dma((KH,)),
            dma((1,)), dma((KH,)), dma((KH,)), dma((KH,)), dma((1,)),
        ],
        compiler_params=pltpu.CompilerParams(
            collective_id=0, has_side_effects=True, vmem_limit_bytes=44 * 2**20
        ),
    )(
        *(
            pltpu.with_memory_space_constraint(a, pltpu.HBM)
            for a in (
                query_rows, key_rows, value_rows, grad_out,
                order, recv_place.reshape(1, T), doc_ids,
            )
        )
    )
    return pl.pallas_call(
        home,
        out_shape=tuple(jax.ShapeDtypeStruct(s, BF) for s in (wide, wide, thin, thin)),
        in_specs=[vmem] * 3,
        out_specs=(hbm,) * 4,
        scratch_shapes=[
            vm((KH, T, 2 * GW), BF), vm(thin, BF), vm(thin, BF), dma((2 * KH + 2,)),
        ],
        compiler_params=pltpu.CompilerParams(vmem_limit_bytes=16 * 2**20),
    )(order, rows_back, keys_back)


def solution(mesh):
    rows = P(("dp", "ctx"), None)
    return jax.shard_map(
        body,
        mesh=mesh,
        in_specs=(rows,) * 4 + (P("dp", "ctx", None),) * 2 + (P("dp", None),),
        out_specs=(rows,) * 4,
        check_vma=False,
    )
```

```python
import jax
import jax.numpy as jnp
from jax import lax
from jax.experimental import pallas as pl
from jax.experimental.pallas import tpu as pltpu
from jax.sharding import PartitionSpec as P

BF, F32, I32 = jnp.bfloat16, jnp.float32, jnp.int32
MESH = pl.DeviceIdType.MESH
HD = 128
KH = 4
GS = 8
T = 128
NDP = 8
SHARE = T // NDP
NCH = 9
W = NCH * T
GW = GS * HD
SCALE = HD**-0.5
SCALE2 = SCALE * 1.4426950408889634
NEG = -1e30
NT = (((1,), (1,)), ((), ()))
NN = (((1,), (0,)), ((), ()))
Y_MSGS = ((1, 0), (2, 0), (3, 0), (1, 1), (3, 1))
LAG = 1
KEYS_DIRECT = ()
GRADS_DIRECT = (3,)


def dot(a, b, dims=NN):
    return lax.dot_general(a, b, dims, preferred_element_type=F32)


def kernel(
    q_hbm, k_hbm, v_hbm, g_hbm, order_hbm, place_hbm, doc_hbm,
    odr, zkr,
    q_in, g_in, k_in, v_in, hot, nat, nat_t,
    kvs, kvr, qgs, qgr, kv, bias, kt, vt,
    ods, dkv, y2s, yrec, x6rec, acc, xs, xrec, zks,
    probs, probs_b, dscore, delta, order_ref, place_ref, doc_ref, in_sem, own_sem, sent, kv_rs, qg_rs, x_rs, x6_rs, y_rs, y2_rs,
    od_rs, yr_rs, xr_rs, xr6_rs, zk_rs,
):
    d = lax.axis_index("dp")
    c = lax.axis_index("ctx")
    x, y = c // 4, c % 4

    def group_at(j):
        return (lax.rem(d + j, NDP), c)

    def x_at(j):
        return (d, lax.rem(x + j + 4, 4) * 4 + y)

    def y_at(j):
        return (d, x * 4 + lax.rem(y + j + 4, 4))

    bar = pltpu.get_barrier_semaphore()
    friends = [group_at(j) for j in range(1, NDP)]
    friends += [x_at(j) for j in range(1, 4)] + [y_at(j) for j in range(1, 4)]
    for f in friends:
        pl.semaphore_signal(bar, 1, device_id=f, device_id_type=MESH)

    pairs = (
        (order_hbm, order_ref), (k_hbm, k_in), (v_hbm, v_in), (place_hbm, place_ref),
        (doc_hbm, doc_ref), (q_hbm, q_in), (g_hbm, g_in),
    )
    arrivals = [pltpu.make_async_copy(a, b, in_sem.at[n]) for n, (a, b) in enumerate(pairs)]
    for cp in arrivals:
        cp.start()

    rows = lax.broadcasted_iota(I32, (T, T), 0)
    arrivals[0].wait()
    hot[...] = (rows == order_ref[...]).astype(F32).T.astype(BF)
    mine = pl.ds(pl.multiple_of(d * SHARE, SHARE), SHARE)

    def part(j):
        return pl.ds(pl.multiple_of(lax.rem(d + j, NDP) * SHARE, SHARE), SHARE)

    def rcopy(src, dst, ss, rs, to):
        return pltpu.make_async_remote_copy(
            src_ref=src, dst_ref=dst, send_sem=ss, recv_sem=rs, device_id=to, device_id_type=MESH
        )

    def a2a(src, dst, sem, rs, j):
        return rcopy(src.at[part(j)], dst.at[mine], sent.at[sem], rs, group_at(j))

    def kv_copy(g, j):
        return a2a(kvs.at[g], kvr.at[g], 0, kv_rs.at[g], j)

    def qg_copy(g, j):
        return a2a(qgs.at[g], qgr.at[g], 1, qg_rs.at[g], j)

    def od_copy(g, j):
        return a2a(ods.at[g], odr.at[g], 2, od_rs.at[0], j)

    def zk_copy(g, j):
        return a2a(zks.at[g], zkr.at[g], 3, zk_rs.at[0], j)

    def landed(ref, rs):
        rcopy(ref, ref, sent.at[0], rs, group_at(1)).wait_recv()

    def left(ref, sem):
        rcopy(ref, ref, sent.at[sem], kv_rs.at[0], group_at(1)).wait_send()

    def chunk(o):
        return pl.ds(pl.multiple_of(o * T, T), T)

    def x_copy(g, j):
        return rcopy(
            kv.at[g, chunk(0)], kv.at[g, chunk(4 * j)], sent.at[4], x_rs.at[g], x_at(j)
        )

    def x_relay(g):
        return rcopy(kv.at[g, chunk(2)], kv.at[g, chunk(6)], sent.at[8], x6_rs.at[g], x_at(1))

    def y_direct(g):
        src = 4 * ((y + 2) // 4 + 1)
        return rcopy(kv.at[g, chunk(src)], kv.at[g, chunk(6)], sent.at[8], x6_rs.at[g], y_at(2))

    def yr_direct(g, j):
        if j == 6:
            return rcopy(dkv.at[g, chunk(6)], x6rec.at[g], sent.at[9], xr6_rs.at[g], y_at(-2))
        at = chunk(Y_MSGS.index((2, 0)))
        return rcopy(
            dkv.at[g, chunk(2)], yrec.at[g, at], sent.at[6], yr_rs.at[g], y_at(-2)
        )

    def grads_direct(g):
        flag = g < 0
        for n in GRADS_DIRECT:
            flag |= g == n
        return flag

    def y_copy(g, j, b):
        src = 4 * ((y + j) // 4 + b)
        rs = (y2_rs if (j, b) == (2, 0) else y_rs).at[g]
        return rcopy(kv.at[g, chunk(src)], kv.at[g, chunk(j + 4 * b)], sent.at[5], rs, y_at(j))

    def yr_copy(g, j, b):
        src = y2s.at[g] if (j, b) == (2, 0) else dkv.at[g, chunk(j + 4 * b)]
        return rcopy(src, yrec.at[g, chunk(Y_MSGS.index((j, b)))], sent.at[6], yr_rs.at[g], y_at(-j))

    def xr_relay(g):
        return rcopy(dkv.at[g, chunk(6)], x6rec.at[g], sent.at[9], xr6_rs.at[g], x_at(-1))

    def xr_copy(g, j):
        return rcopy(
            xs.at[g, chunk(j - 1)], xrec.at[g, chunk(j - 1)], sent.at[7], xr_rs.at[g], x_at(-j)
        )

    def own_od():
        return pltpu.make_async_copy(ods.at[:, mine], odr.at[:, mine], own_sem.at[0])

    def own_zk():
        return pltpu.make_async_copy(zks.at[:, mine], zkr.at[:, mine], own_sem.at[1])

    arrivals[1].wait()
    arrivals[2].wait()
    for g in range(KH):
        cols = slice(g * HD, (g + 1) * HD)
        kvs[g, :, 0:HD] = dot(hot[...], k_in[:, cols]).astype(BF)
        kvs[g, :, HD : 2 * HD] = dot(hot[...], v_in[:, cols]).astype(BF)
    kvr[:, mine, :] = kvs[:, mine, :]
    pl.semaphore_wait(bar, len(friends))
    for g in range(KH):
        for j in range(1, NDP):
            kv_copy(g, j).start()

    arrivals[5].wait()
    arrivals[6].wait()

    def send_rows(g, carry):
        cols = pl.ds(pl.multiple_of(g * GW, GW), GW)
        qgs[g, :, 0:GW] = dot(hot[...], q_in[:, cols]).astype(BF)
        qgs[g, :, GW : 2 * GW] = dot(hot[...], g_in[:, cols]).astype(BF)
        qgr[g, mine, :] = qgs[g, mine, :]
        for j in range(1, NDP):
            qg_copy(g, j).start()
        return carry

    lax.fori_loop(0, KH, send_rows, 0)

    arrivals[3].wait()
    nat32 = (rows == place_ref[...]).astype(F32)
    nat[...] = nat32.astype(BF)
    nat_t[...] = nat32.T.astype(BF)

    def masks():
        arrivals[4].wait()
        q_pos = place_ref[...]
        own_doc = doc_ref[0:1, pl.ds(pl.multiple_of(c * T, T), T)].astype(F32).astype(BF)
        q_doc = dot(jnp.broadcast_to(own_doc, (8, T)), nat[...])[0:1]

        def mask(o, carry):
            at = lax.rem(c - o + 16, 16)
            row = doc_ref[0:1, pl.ds(pl.multiple_of(at * T, T), T)].astype(F32)
            k_doc = jnp.broadcast_to(row, (T, T)).T
            ahead = jnp.where(o == 0, rows - q_pos, 0)
            ahead = jnp.where(o <= c, ahead, 1)
            bias[chunk(o), :] = jnp.where((k_doc == q_doc) & (ahead <= 0), 0.0, NEG)
            return carry

        lax.fori_loop(0, NCH, mask, 0)

    others = pl.ds(0, T - SHARE)
    def own(g):
        landed(kvr.at[g, others], kv_rs.at[g])
        kv[g, 0:T, :] = dot(nat[...], kvr[g]).astype(BF)
        for j in (1, 2):
            x_copy(g, j).start()

    def early(g):
        for j in (2, 1, 3):
            pl.when(y + j < 4)(y_copy(g, j, 0).start)

    def late(g):
        landed(kv.at[g, pl.ds(0, 2 * T)], x_rs.at[g])
        for j in (2, 1, 3):
            pl.when(y + j >= 4)(y_copy(g, j, 0).start)
        for j in (1, 3):
            y_copy(g, j, 1).start()
        if g in KEYS_DIRECT:
            y_direct(g).start()

    def relay(g):
        landed(kv.at[g, pl.ds(0, T)], y2_rs.at[g])
        if g not in KEYS_DIRECT:
            x_relay(g).start()

    own(0)
    early(0)
    own(1)
    late(0)
    early(1)
    masks()
    relay(0)
    late(1)
    own(2)
    early(2)

    def stacked(g, at):
        return jnp.concatenate(
            [qgr[g, :, at + h * HD : at + (h + 1) * HD] for h in range(GS)], axis=0
        )

    def spread(g, at, rows):
        for h in range(GS):
            ods[g, :, at + h * HD : at + (h + 1) * HD] = rows[h * T : (h + 1) * T]

    def attend(g):
        landed(qgr.at[g, others], qg_rs.at[g])
        landed(kv.at[g, pl.ds(0, 4 * T)], y_rs.at[g])
        landed(kv.at[g, pl.ds(0, T)], x6_rs.at[g])
        kt[...] = kv[g, :, 0:HD].T
        vt[...] = kv[g, :, HD : 2 * HD].T
        scores = dot(kv[g, :, 0:HD], stacked(g, 0), NT) * SCALE2
        scores += jnp.concatenate([bias[...]] * GS, axis=1)
        weights = jnp.exp2(scores - jnp.max(scores, axis=0, keepdims=True))
        held = weights * (1.0 / jnp.sum(weights, axis=0, keepdims=True))
        probs[...] = held
        probs_b[...] = held.astype(BF)
        out = dot(vt[...], probs_b[...]).astype(BF)
        delta[...] = jnp.sum(
            out.astype(F32) * stacked(g, GW).T.astype(F32), axis=0, keepdims=True
        )
        spread(g, 0, out.T)

    def key_grads(g):
        prob_grad = dot(kv[g, :, HD : 2 * HD], stacked(g, GW), NT)
        dscore[...] = (probs[...] * (prob_grad - delta[...])).astype(BF)
        dkv[g, :, 0:HD] = (dot(dscore[...], stacked(g, 0)) * SCALE).astype(BF)
        dkv[g, :, HD : 2 * HD] = dot(probs_b[...], stacked(g, GW)).astype(BF)
        pl.when(jnp.logical_not(grads_direct(g)))(xr_relay(g).start)

        @pl.when(grads_direct(g))
        def _():
            yr_direct(g, 2).start()
            yr_direct(g, 6).start()

        for j, b in ((1, 0), (3, 0), (1, 1), (3, 1)):
            yr_copy(g, j, b).start()

    def query_grads(g):
        spread(g, GW, (dot(kt[...], dscore[...]) * SCALE).astype(BF).T)
        for j in range(1, NDP):
            od_copy(g, j).start()

    def add_relayed(g):
        @pl.when(jnp.logical_not(grads_direct(g)))
        def _():
            landed(x6rec.at[g], xr6_rs.at[g])
            there = dkv[g, 2 * T : 3 * T, :].astype(F32) + x6rec[g].astype(F32)
            y2s[g] = there.astype(BF)
            yr_copy(g, 2, 0).start()

    def add_y(g):
        for k in range(3):
            acc[g, k] = dkv[g, 4 * k * T : (4 * k + 1) * T, :].astype(F32)
        landed(yrec.at[g], yr_rs.at[g])
        for n, (j, b) in enumerate(Y_MSGS):
            acc[g, (y + j) // 4 + b] += yrec[g, n * T : (n + 1) * T, :].astype(F32)

        @pl.when(grads_direct(g))
        def _():
            landed(x6rec.at[g], xr6_rs.at[g])
            acc[g, (y + 2) // 4 + 1] += x6rec[g].astype(F32)

        for j in (1, 2):
            xs[g, (j - 1) * T : j * T, :] = acc[g, j].astype(BF)
            xr_copy(g, j).start()

    def add_x(g):
        landed(xrec.at[g], xr_rs.at[g])
        total = acc[g, 0]
        for j in (1, 2):
            total += xrec[g, (j - 1) * T : j * T, :].astype(F32)
        zks[g] = dot(nat_t[...], total.astype(BF)).astype(BF)
        for j in range(1, NDP):
            zk_copy(g, j).start()

    def turn(t, carry):
        def later(steps):
            for step, lag in steps:
                pl.when((t >= lag) & (t < KH + lag))(lambda step=step, lag=lag: step(t - lag))

        @pl.when(t < KH)
        def _():
            attend(t)

            @pl.when(t == 0)
            def _():
                relay(1)
                late(2)
                own(3)
                early(3)

            @pl.when(t == 1)
            def _():
                late(3)
                relay(2)

            pl.when(t == 2)(lambda: relay(3))

        later(((add_relayed, LAG),))
        pl.when(t < KH)(lambda: key_grads(t))
        later(((add_y, LAG + 1),(add_x, LAG + 2),))
        pl.when(t < KH)(lambda: query_grads(t))
        return carry

    lax.fori_loop(0, KH + LAG + 2, turn, 0)

    own_od().start()
    own_zk().start()
    left(kvs.at[:, others], 0)
    left(qgs.at[:, others], 1)
    left(ods.at[:, others], 2)
    left(zks.at[:, others], 3)
    left(kv.at[:, pl.ds(0, 2 * T)], 4)
    left(kv.at[:, pl.ds(0, T)], 8)
    left(kv.at[:, pl.ds(0, T)], 9)
    left(yrec, 5)
    left(yrec, 6)
    left(kv.at[:, pl.ds(0, 2 * T)], 7)
    landed(odr.at[:, others], od_rs.at[0])
    landed(zkr.at[:, others], zk_rs.at[0])
    own_od().wait()
    own_zk().wait()


def home(order_ref, od, zk, out_hbm, dq_hbm, dk_hbm, dv_hbm, res, gk, gv, sem):
    def leave(g):
        cols = pl.ds(g * GW, GW)
        return (
            pltpu.make_async_copy(res.at[g, :, pl.ds(0, GW)], out_hbm.at[:, cols], sem.at[g]),
            pltpu.make_async_copy(res.at[g, :, pl.ds(GW, GW)], dq_hbm.at[:, cols], sem.at[KH + g]),
        )

    rows = lax.broadcasted_iota(I32, (T, T), 0)
    back = (rows == order_ref[...]).astype(F32).astype(BF)
    for g in range(KH):
        res[g] = dot(back, od[g]).astype(BF)
        for cp in leave(g):
            cp.start()
    for g in range(KH):
        grads = dot(back, zk[g]).astype(BF)
        gk[:, g * HD : (g + 1) * HD] = grads[:, 0:HD]
        gv[:, g * HD : (g + 1) * HD] = grads[:, HD : 2 * HD]
    ends = [pltpu.make_async_copy(gk, dk_hbm, sem.at[2 * KH])]
    ends.append(pltpu.make_async_copy(gv, dv_hbm, sem.at[2 * KH + 1]))
    for cp in ends:
        cp.start()
    for g in range(KH):
        for cp in leave(g):
            cp.wait()
    for cp in ends:
        cp.wait()


def body(query_rows, key_rows, value_rows, grad_out, send_order, recv_place, doc_ids):
    vm = pltpu.VMEM
    dma = pltpu.SemaphoreType.DMA
    hbm = pl.BlockSpec(memory_space=pl.ANY)
    vmem = pl.BlockSpec(memory_space=pltpu.VMEM)
    wide, thin = (T, KH * GW), (T, KH * HD)
    order = send_order.reshape(1, T)
    rows_back, keys_back = pl.pallas_call(
        kernel,
        out_shape=(
            jax.ShapeDtypeStruct((KH, T, 2 * GW), BF),
            jax.ShapeDtypeStruct((KH, T, 2 * HD), BF),
        ),
        in_specs=[hbm] * 7,
        out_specs=(hbm,) * 2,
        scratch_shapes=[
            vm(wide, BF), vm(wide, BF), vm(thin, BF), vm(thin, BF),
            vm((T, T), BF), vm((T, T), BF), vm((T, T), BF),
            vm((KH, T, 2 * HD), BF), vm((KH, T, 2 * HD), BF),
            vm((KH, T, 2 * GW), BF), vm((KH, T, 2 * GW), BF),
            vm((KH, W, 2 * HD), BF), vm((W, T), F32), vm((HD, W), BF), vm((HD, W), BF),
            vm((KH, T, 2 * GW), BF), vm((KH, W, 2 * HD), BF),
            vm((KH, T, 2 * HD), BF), vm((KH, 5 * T, 2 * HD), BF), vm((KH, T, 2 * HD), BF),
            vm((KH, 3, T, 2 * HD), F32), vm((KH, 2 * T, 2 * HD), BF), vm((KH, 2 * T, 2 * HD), BF),
            vm((KH, T, 2 * HD), BF),
            vm((W, GW), F32), vm((W, GW), BF), vm((W, GW), BF), vm((1, GW), F32),
            vm((1, T), I32), vm((1, T), I32), vm(doc_ids.shape, I32), dma((7,)), dma((2,)),
            dma((10,)), dma((KH,)), dma((KH,)), dma((KH,)), dma((KH,)), dma((KH,)), dma((KH,)),
            dma((1,)), dma((KH,)), dma((KH,)), dma((KH,)), dma((1,)),
        ],
        compiler_params=pltpu.CompilerParams(
            collective_id=0, has_side_effects=True, vmem_limit_bytes=44 * 2**20
        ),
    )(
        *(
            pltpu.with_memory_space_constraint(a, pltpu.HBM)
            for a in (
                query_rows, key_rows, value_rows, grad_out,
                order, recv_place.reshape(1, T), doc_ids,
            )
        )
    )
    return pl.pallas_call(
        home,
        out_shape=tuple(jax.ShapeDtypeStruct(s, BF) for s in (wide, wide, thin, thin)),
        in_specs=[vmem] * 3,
        out_specs=(hbm,) * 4,
        scratch_shapes=[
            vm((KH, T, 2 * GW), BF), vm(thin, BF), vm(thin, BF), dma((2 * KH + 2,)),
        ],
        compiler_params=pltpu.CompilerParams(vmem_limit_bytes=16 * 2**20),
    )(order, rows_back, keys_back)


def solution(mesh):
    rows = P(("dp", "ctx"), None)
    return jax.shard_map(
        body,
        mesh=mesh,
        in_specs=(rows,) * 4 + (P("dp", "ctx", None),) * 2 + (P("dp", None),),
        out_specs=(rows,) * 4,
        check_vma=False,
    )
```

```python
import jax
import jax.numpy as jnp
from jax import lax
from jax.experimental import pallas as pl
from jax.experimental.pallas import tpu as pltpu
from jax.sharding import PartitionSpec as P

BF, F32, I32 = jnp.bfloat16, jnp.float32, jnp.int32
MESH = pl.DeviceIdType.MESH
HD = 128
KH = 4
GS = 8
T = 128
NDP = 8
SHARE = T // NDP
NCH = 9
W = NCH * T
GW = GS * HD
SCALE = HD**-0.5
SCALE2 = SCALE * 1.4426950408889634
NEG = -1e30
NT = (((1,), (1,)), ((), ()))
NN = (((1,), (0,)), ((), ()))
Y_MSGS = ((1, 0), (2, 0), (3, 0), (1, 1), (3, 1))
LAG = 1
KEYS_DIRECT = ()
GRADS_DIRECT = (3,)


def dot(a, b, dims=NN):
    return lax.dot_general(a, b, dims, preferred_element_type=F32)


def kernel(
    q_hbm, k_hbm, v_hbm, g_hbm, order_hbm, place_hbm, doc_hbm,
    odr, zkr,
    q_in, g_in, k_in, v_in, hot, nat, nat_t,
    kvs, kvr, qgs, qgr, kv, bias, kt, vt,
    ods, dkv, y2s, yrec, x6rec, acc, xs, xrec, zks,
    probs, probs_b, dscore, delta, order_ref, place_ref, doc_ref, in_sem, own_sem, sent, kv_rs, qg_rs, x_rs, x6_rs, y_rs, y2_rs,
    od_rs, yr_rs, xr_rs, xr6_rs, zk_rs,
):
    d = lax.axis_index("dp")
    c = lax.axis_index("ctx")
    x, y = c // 4, c % 4

    def group_at(j):
        return (lax.rem(d + j, NDP), c)

    def x_at(j):
        return (d, lax.rem(x + j + 4, 4) * 4 + y)

    def y_at(j):
        return (d, x * 4 + lax.rem(y + j + 4, 4))

    bar = pltpu.get_barrier_semaphore()
    friends = [group_at(j) for j in range(1, NDP)]
    friends += [x_at(j) for j in range(1, 4)] + [y_at(j) for j in range(1, 4)]
    for f in friends:
        pl.semaphore_signal(bar, 1, device_id=f, device_id_type=MESH)

    pairs = (
        (order_hbm, order_ref), (k_hbm, k_in), (v_hbm, v_in), (place_hbm, place_ref),
        (doc_hbm, doc_ref), (q_hbm, q_in), (g_hbm, g_in),
    )
    arrivals = [pltpu.make_async_copy(a, b, in_sem.at[n]) for n, (a, b) in enumerate(pairs)]
    for cp in arrivals:
        cp.start()

    rows = lax.broadcasted_iota(I32, (T, T), 0)
    arrivals[0].wait()
    hot[...] = (rows == order_ref[...]).astype(F32).T.astype(BF)
    mine = pl.ds(pl.multiple_of(d * SHARE, SHARE), SHARE)

    def part(j):
        return pl.ds(pl.multiple_of(lax.rem(d + j, NDP) * SHARE, SHARE), SHARE)

    def rcopy(src, dst, ss, rs, to):
        return pltpu.make_async_remote_copy(
            src_ref=src, dst_ref=dst, send_sem=ss, recv_sem=rs, device_id=to, device_id_type=MESH
        )

    def a2a(src, dst, sem, rs, j):
        return rcopy(src.at[part(j)], dst.at[mine], sent.at[sem], rs, group_at(j))

    def kv_copy(g, j):
        return a2a(kvs.at[g], kvr.at[g], 0, kv_rs.at[g], j)

    def qg_copy(g, j):
        return a2a(qgs.at[g], qgr.at[g], 1, qg_rs.at[g], j)

    def od_copy(g, j):
        return a2a(ods.at[g], odr.at[g], 2, od_rs.at[0], j)

    def zk_copy(g, j):
        return a2a(zks.at[g], zkr.at[g], 3, zk_rs.at[0], j)

    def landed(ref, rs):
        rcopy(ref, ref, sent.at[0], rs, group_at(1)).wait_recv()

    def left(ref, sem):
        rcopy(ref, ref, sent.at[sem], kv_rs.at[0], group_at(1)).wait_send()

    def chunk(o):
        return pl.ds(pl.multiple_of(o * T, T), T)

    def x_copy(g, j):
        return rcopy(
            kv.at[g, chunk(0)], kv.at[g, chunk(4 * j)], sent.at[4], x_rs.at[g], x_at(j)
        )

    def x_relay(g):
        return rcopy(kv.at[g, chunk(2)], kv.at[g, chunk(6)], sent.at[8], x6_rs.at[g], x_at(1))

    def y_direct(g):
        src = 4 * ((y + 2) // 4 + 1)
        return rcopy(kv.at[g, chunk(src)], kv.at[g, chunk(6)], sent.at[8], x6_rs.at[g], y_at(2))

    def yr_direct(g, j):
        if j == 6:
            return rcopy(dkv.at[g, chunk(6)], x6rec.at[g], sent.at[9], xr6_rs.at[g], y_at(-2))
        at = chunk(Y_MSGS.index((2, 0)))
        return rcopy(
            dkv.at[g, chunk(2)], yrec.at[g, at], sent.at[6], yr_rs.at[g], y_at(-2)
        )

    def grads_direct(g):
        flag = g < 0
        for n in GRADS_DIRECT:
            flag |= g == n
        return flag

    def y_copy(g, j, b):
        src = 4 * ((y + j) // 4 + b)
        rs = (y2_rs if (j, b) == (2, 0) else y_rs).at[g]
        return rcopy(kv.at[g, chunk(src)], kv.at[g, chunk(j + 4 * b)], sent.at[5], rs, y_at(j))

    def yr_copy(g, j, b):
        src = y2s.at[g] if (j, b) == (2, 0) else dkv.at[g, chunk(j + 4 * b)]
        return rcopy(src, yrec.at[g, chunk(Y_MSGS.index((j, b)))], sent.at[6], yr_rs.at[g], y_at(-j))

    def xr_relay(g):
        return rcopy(dkv.at[g, chunk(6)], x6rec.at[g], sent.at[9], xr6_rs.at[g], x_at(-1))

    def xr_copy(g, j):
        return rcopy(
            xs.at[g, chunk(j - 1)], xrec.at[g, chunk(j - 1)], sent.at[7], xr_rs.at[g], x_at(-j)
        )

    def own_od():
        return pltpu.make_async_copy(ods.at[:, mine], odr.at[:, mine], own_sem.at[0])

    def own_zk():
        return pltpu.make_async_copy(zks.at[:, mine], zkr.at[:, mine], own_sem.at[1])

    arrivals[1].wait()
    arrivals[2].wait()
    for g in range(KH):
        cols = slice(g * HD, (g + 1) * HD)
        kvs[g, :, 0:HD] = dot(hot[...], k_in[:, cols]).astype(BF)
        kvs[g, :, HD : 2 * HD] = dot(hot[...], v_in[:, cols]).astype(BF)
    kvr[:, mine, :] = kvs[:, mine, :]
    pl.semaphore_wait(bar, len(friends))
    for g in range(KH):
        for j in range(1, NDP):
            kv_copy(g, j).start()

    arrivals[5].wait()
    arrivals[6].wait()

    def send_rows(g, carry):
        cols = pl.ds(pl.multiple_of(g * GW, GW), GW)
        qgs[g, :, 0:GW] = dot(hot[...], q_in[:, cols]).astype(BF)
        qgs[g, :, GW : 2 * GW] = dot(hot[...], g_in[:, cols]).astype(BF)
        qgr[g, mine, :] = qgs[g, mine, :]
        for j in range(1, NDP):
            qg_copy(g, j).start()
        return carry

    lax.fori_loop(0, KH, send_rows, 0)

    arrivals[3].wait()
    nat32 = (rows == place_ref[...]).astype(F32)
    nat[...] = nat32.astype(BF)
    nat_t[...] = nat32.T.astype(BF)

    def masks():
        arrivals[4].wait()
        q_pos = place_ref[...]
        own_doc = doc_ref[0:1, pl.ds(pl.multiple_of(c * T, T), T)].astype(F32).astype(BF)
        q_doc = dot(jnp.broadcast_to(own_doc, (8, T)), nat[...])[0:1]

        def mask(o, carry):
            at = lax.rem(c - o + 16, 16)
            row = doc_ref[0:1, pl.ds(pl.multiple_of(at * T, T), T)].astype(F32)
            k_doc = jnp.broadcast_to(row, (T, T)).T
            ahead = jnp.where(o == 0, rows - q_pos, 0)
            ahead = jnp.where(o <= c, ahead, 1)
            bias[chunk(o), :] = jnp.where((k_doc == q_doc) & (ahead <= 0), 0.0, NEG)
            return carry

        lax.fori_loop(0, NCH, mask, 0)

    others = pl.ds(0, T - SHARE)
    def own(g):
        landed(kvr.at[g, others], kv_rs.at[g])
        kv[g, 0:T, :] = dot(nat[...], kvr[g]).astype(BF)
        for j in (2, 1):
            x_copy(g, j).start()

    def early(g):
        for j in (2, 1, 3):
            pl.when(y + j < 4)(y_copy(g, j, 0).start)

    def late(g):
        landed(kv.at[g, pl.ds(0, 2 * T)], x_rs.at[g])
        for j in (2, 1, 3):
            pl.when(y + j >= 4)(y_copy(g, j, 0).start)
        for j in (1, 3):
            y_copy(g, j, 1).start()
        if g in KEYS_DIRECT:
            y_direct(g).start()

    def relay(g):
        landed(kv.at[g, pl.ds(0, T)], y2_rs.at[g])
        if g not in KEYS_DIRECT:
            x_relay(g).start()

    own(0)
    early(0)
    own(1)
    late(0)
    early(1)
    masks()
    relay(0)
    late(1)
    own(2)
    early(2)

    def stacked(g, at):
        return jnp.concatenate(
            [qgr[g, :, at + h * HD : at + (h + 1) * HD] for h in range(GS)], axis=0
        )

    def spread(g, at, rows):
        for h in range(GS):
            ods[g, :, at + h * HD : at + (h + 1) * HD] = rows[h * T : (h + 1) * T]

    def attend(g):
        landed(qgr.at[g, others], qg_rs.at[g])
        landed(kv.at[g, pl.ds(0, 4 * T)], y_rs.at[g])
        landed(kv.at[g, pl.ds(0, T)], x6_rs.at[g])
        kt[...] = kv[g, :, 0:HD].T
        vt[...] = kv[g, :, HD : 2 * HD].T
        scores = dot(kv[g, :, 0:HD], stacked(g, 0), NT) * SCALE2
        scores += jnp.concatenate([bias[...]] * GS, axis=1)
        weights = jnp.exp2(scores - jnp.max(scores, axis=0, keepdims=True))
        held = weights * (1.0 / jnp.sum(weights, axis=0, keepdims=True))
        probs[...] = held
        probs_b[...] = held.astype(BF)
        out = dot(vt[...], probs_b[...]).astype(BF)
        delta[...] = jnp.sum(
            out.astype(F32) * stacked(g, GW).T.astype(F32), axis=0, keepdims=True
        )
        spread(g, 0, out.T)

    def key_grads(g):
        prob_grad = dot(kv[g, :, HD : 2 * HD], stacked(g, GW), NT)
        dscore[...] = (probs[...] * (prob_grad - delta[...])).astype(BF)
        dkv[g, :, 0:HD] = (dot(dscore[...], stacked(g, 0)) * SCALE).astype(BF)
        dkv[g, :, HD : 2 * HD] = dot(probs_b[...], stacked(g, GW)).astype(BF)
        pl.when(jnp.logical_not(grads_direct(g)))(xr_relay(g).start)

        @pl.when(grads_direct(g))
        def _():
            yr_direct(g, 2).start()
            yr_direct(g, 6).start()

        for j, b in ((1, 0), (3, 0), (1, 1), (3, 1)):
            yr_copy(g, j, b).start()

    def query_grads(g):
        spread(g, GW, (dot(kt[...], dscore[...]) * SCALE).astype(BF).T)
        for j in range(1, NDP):
            od_copy(g, j).start()

    def add_relayed(g):
        @pl.when(jnp.logical_not(grads_direct(g)))
        def _():
            landed(x6rec.at[g], xr6_rs.at[g])
            there = dkv[g, 2 * T : 3 * T, :].astype(F32) + x6rec[g].astype(F32)
            y2s[g] = there.astype(BF)
            yr_copy(g, 2, 0).start()

    def add_y(g):
        for k in range(3):
            acc[g, k] = dkv[g, 4 * k * T : (4 * k + 1) * T, :].astype(F32)
        landed(yrec.at[g], yr_rs.at[g])
        for n, (j, b) in enumerate(Y_MSGS):
            acc[g, (y + j) // 4 + b] += yrec[g, n * T : (n + 1) * T, :].astype(F32)

        @pl.when(grads_direct(g))
        def _():
            landed(x6rec.at[g], xr6_rs.at[g])
            acc[g, (y + 2) // 4 + 1] += x6rec[g].astype(F32)

        for j in (2, 1):
            xs[g, (j - 1) * T : j * T, :] = acc[g, j].astype(BF)
            xr_copy(g, j).start()

    def add_x(g):
        landed(xrec.at[g], xr_rs.at[g])
        total = acc[g, 0]
        for j in (1, 2):
            total += xrec[g, (j - 1) * T : j * T, :].astype(F32)
        zks[g] = dot(nat_t[...], total.astype(BF)).astype(BF)
        for j in range(1, NDP):
            zk_copy(g, j).start()

    def turn(t, carry):
        def later(steps):
            for step, lag in steps:
                pl.when((t >= lag) & (t < KH + lag))(lambda step=step, lag=lag: step(t - lag))

        @pl.when(t < KH)
        def _():
            attend(t)

            @pl.when(t == 0)
            def _():
                relay(1)
                late(2)
                own(3)
                early(3)

            @pl.when(t == 1)
            def _():
                late(3)
                relay(2)

            pl.when(t == 2)(lambda: relay(3))

        later(((add_relayed, LAG),))
        pl.when(t < KH)(lambda: key_grads(t))
        later(((add_y, LAG + 1),(add_x, LAG + 2),))
        pl.when(t < KH)(lambda: query_grads(t))
        return carry

    lax.fori_loop(0, KH + LAG + 2, turn, 0)

    own_od().start()
    own_zk().start()
    left(kvs.at[:, others], 0)
    left(qgs.at[:, others], 1)
    left(ods.at[:, others], 2)
    left(zks.at[:, others], 3)
    left(kv.at[:, pl.ds(0, 2 * T)], 4)
    left(kv.at[:, pl.ds(0, T)], 8)
    left(kv.at[:, pl.ds(0, T)], 9)
    left(yrec, 5)
    left(yrec, 6)
    left(kv.at[:, pl.ds(0, 2 * T)], 7)
    landed(odr.at[:, others], od_rs.at[0])
    landed(zkr.at[:, others], zk_rs.at[0])
    own_od().wait()
    own_zk().wait()


def home(order_ref, od, zk, out_hbm, dq_hbm, dk_hbm, dv_hbm, res, gk, gv, sem):
    def leave(g):
        cols = pl.ds(g * GW, GW)
        return (
            pltpu.make_async_copy(res.at[g, :, pl.ds(0, GW)], out_hbm.at[:, cols], sem.at[g]),
            pltpu.make_async_copy(res.at[g, :, pl.ds(GW, GW)], dq_hbm.at[:, cols], sem.at[KH + g]),
        )

    rows = lax.broadcasted_iota(I32, (T, T), 0)
    back = (rows == order_ref[...]).astype(F32).astype(BF)
    for g in range(KH):
        res[g] = dot(back, od[g]).astype(BF)
        for cp in leave(g):
            cp.start()
    for g in range(KH):
        grads = dot(back, zk[g]).astype(BF)
        gk[:, g * HD : (g + 1) * HD] = grads[:, 0:HD]
        gv[:, g * HD : (g + 1) * HD] = grads[:, HD : 2 * HD]
    ends = [pltpu.make_async_copy(gk, dk_hbm, sem.at[2 * KH])]
    ends.append(pltpu.make_async_copy(gv, dv_hbm, sem.at[2 * KH + 1]))
    for cp in ends:
        cp.start()
    for g in range(KH):
        for cp in leave(g):
            cp.wait()
    for cp in ends:
        cp.wait()


def body(query_rows, key_rows, value_rows, grad_out, send_order, recv_place, doc_ids):
    vm = pltpu.VMEM
    dma = pltpu.SemaphoreType.DMA
    hbm = pl.BlockSpec(memory_space=pl.ANY)
    vmem = pl.BlockSpec(memory_space=pltpu.VMEM)
    wide, thin = (T, KH * GW), (T, KH * HD)
    order = send_order.reshape(1, T)
    rows_back, keys_back = pl.pallas_call(
        kernel,
        out_shape=(
            jax.ShapeDtypeStruct((KH, T, 2 * GW), BF),
            jax.ShapeDtypeStruct((KH, T, 2 * HD), BF),
        ),
        in_specs=[hbm] * 7,
        out_specs=(hbm,) * 2,
        scratch_shapes=[
            vm(wide, BF), vm(wide, BF), vm(thin, BF), vm(thin, BF),
            vm((T, T), BF), vm((T, T), BF), vm((T, T), BF),
            vm((KH, T, 2 * HD), BF), vm((KH, T, 2 * HD), BF),
            vm((KH, T, 2 * GW), BF), vm((KH, T, 2 * GW), BF),
            vm((KH, W, 2 * HD), BF), vm((W, T), F32), vm((HD, W), BF), vm((HD, W), BF),
            vm((KH, T, 2 * GW), BF), vm((KH, W, 2 * HD), BF),
            vm((KH, T, 2 * HD), BF), vm((KH, 5 * T, 2 * HD), BF), vm((KH, T, 2 * HD), BF),
            vm((KH, 3, T, 2 * HD), F32), vm((KH, 2 * T, 2 * HD), BF), vm((KH, 2 * T, 2 * HD), BF),
            vm((KH, T, 2 * HD), BF),
            vm((W, GW), F32), vm((W, GW), BF), vm((W, GW), BF), vm((1, GW), F32),
            vm((1, T), I32), vm((1, T), I32), vm(doc_ids.shape, I32), dma((7,)), dma((2,)),
            dma((10,)), dma((KH,)), dma((KH,)), dma((KH,)), dma((KH,)), dma((KH,)), dma((KH,)),
            dma((1,)), dma((KH,)), dma((KH,)), dma((KH,)), dma((1,)),
        ],
        compiler_params=pltpu.CompilerParams(
            collective_id=0, has_side_effects=True, vmem_limit_bytes=44 * 2**20
        ),
    )(
        *(
            pltpu.with_memory_space_constraint(a, pltpu.HBM)
            for a in (
                query_rows, key_rows, value_rows, grad_out,
                order, recv_place.reshape(1, T), doc_ids,
            )
        )
    )
    return pl.pallas_call(
        home,
        out_shape=tuple(jax.ShapeDtypeStruct(s, BF) for s in (wide, wide, thin, thin)),
        in_specs=[vmem] * 3,
        out_specs=(hbm,) * 4,
        scratch_shapes=[
            vm((KH, T, 2 * GW), BF), vm(thin, BF), vm(thin, BF), dma((2 * KH + 2,)),
        ],
        compiler_params=pltpu.CompilerParams(vmem_limit_bytes=16 * 2**20),
    )(order, rows_back, keys_back)


def solution(mesh):
    rows = P(("dp", "ctx"), None)
    return jax.shard_map(
        body,
        mesh=mesh,
        in_specs=(rows,) * 4 + (P("dp", "ctx", None),) * 2 + (P("dp", None),),
        out_specs=(rows,) * 4,
        check_vma=False,
    )
```
